768 devices in a mesh: atm: 96 (over z, x, core), ocn: 8 (over y).
Axes of the slice: x: 4, y: 8, z: 12, core: 2. Of those that a mesh axis runs over, the one named last changes fastest.
Arguments:
- atm_fields: bfloat16 [64, 196608], P(None, ('atm', 'ocn')), may hold values from -6 to 6
- ocn_fields: bfloat16 [64, 294912], P(None, ('atm', 'ocn')), may hold values from -6 to 6
- transfer_scale: float32 [64], replicated, may hold values from 0.5 to 2
- atmosphere_slots: int32 [768, 7, 64], P(('atm', 'ocn')), may hold values from -1 to 255, as said below
- ocn_slots: int32 [768, 8, 96], P(('atm', 'ocn')), may hold values from 0 to 383
- xc_ocean: int32 [768, 2, 448], P(('atm', 'ocn')), may hold values from -1 to 767, as said below
- xc_area: bfloat16 [768, 448], P(('atm', 'ocn')), may hold values from 0.19921875 to 1
- xc_theta: bfloat16 [768, 448], P(('atm', 'ocn')), may hold values from 0.099609375 to 0.8984375
Outputs:
- atm_flux: float32 [64, 196608], P(None, ('atm', 'ocn'))
- ocn_flux: float32 [64, 294912], P(None, ('atm', 'ocn'))
The draws below stay inside these ranges and needn't reach their ends.
Inputs may be any that keep to these rules, and one draw needn't show every extreme that they name: `atmosphere_slots`: entry [a2 * 8 + o, k, c] is live (not -1) exactly where xc_ocean[a * 8 + o, 0, k * 64 + c] is, with a = (a2 + k - 3) mod 96; live entries of one block and row come first; each owner receives all 64 slots from its own block (k = 3). `xc_ocean`: both rows are -1 exactly in empty slots, and neither is -1 in live ones.
All inputs are finite; a program needn't handle non-finite values.
Results may differ from the reference program's by a relative error of at most 0.0054.
Values may be sent and summed in bfloat16 or wider, within the bound.
No kernel may reach another device: no remote copies, remote signals or barrier semaphores. Data moves between devices by JAX's collectives and lax.ppermute only.
A program may use at most 32 MiB of HBM per device.

```python
import math
import jax
import jax.numpy as jnp

NF = 64
ATM_DEV = 256
OCN_DEV = 384
RADIUS = 3
SLOT_CAPACITY = 64
OCAP = 96
ITERS = 3
SOURCE_BLOCKS = 7
BLOCKS = 768
ATM_CELLS = 196608
OCN_CELLS = 294912
SLOTS = 448
N_ATM = 96
N_OCN = 8


def owner_live_mask(key):
    counts = jax.random.randint(key, (N_ATM, N_OCN, SOURCE_BLOCKS), SLOT_CAPACITY // 2, SLOT_CAPACITY + 1)
    own_row = jnp.arange(SOURCE_BLOCKS, dtype=jnp.int32)[None, None, :] == RADIUS
    counts = jnp.where(own_row, SLOT_CAPACITY, counts)
    return jnp.arange(SLOT_CAPACITY, dtype=jnp.int32)[None, None, None, :] < counts[..., None]


def draw_atmosphere_slots(key, part):
    live_owner = owner_live_mask(key)
    key = jax.random.fold_in(key, 11)
    atm_ids = jnp.arange(N_ATM, dtype=jnp.int32)
    row_ids = jnp.arange(SOURCE_BLOCKS, dtype=jnp.int32)
    ocean_ids = jnp.arange(N_OCN, dtype=jnp.int32)
    target_of = (atm_ids[:, None] + row_ids[None, :] - RADIUS) % N_ATM
    live_source = live_owner[target_of[:, None, :], ocean_ids[None, :, None], row_ids[None, None, :]]
    cells = jax.random.randint(key, (N_ATM, N_OCN, SOURCE_BLOCKS, SLOT_CAPACITY), 0, ATM_DEV)
    return jnp.where(live_source, cells, -1).reshape(N_ATM * N_OCN, SOURCE_BLOCKS, SLOT_CAPACITY).astype(jnp.int32)


def draw_xc_ocean(key, part):
    slot_count = SOURCE_BLOCKS * SLOT_CAPACITY
    entry_count = N_OCN * OCAP
    live_mask = owner_live_mask(key).reshape(N_ATM * N_OCN, slot_count)
    key = jax.random.fold_in(key, 23)
    keys = jax.random.split(key, N_ATM * N_OCN)
    permutations = jax.vmap(lambda k: jax.random.permutation(k, entry_count))(keys)
    picked_slots = permutations[:, jnp.arange(2 * slot_count, dtype=jnp.int32) % entry_count]
    first_owner = jnp.where(live_mask, picked_slots[:, :slot_count], -1)
    second_owner = jnp.where(live_mask, picked_slots[:, slot_count:], -1)
    return jnp.stack([first_owner, second_owner], axis=1).astype(jnp.int32)


def with_ends(values, rng, least, largest):
    spot = [jax.random.randint(jax.random.fold_in(rng, axis), (), 0, length) for axis, length in enumerate(values.shape)]
    widest = values.shape.index(max(values.shape))
    beside = spot[:widest] + [(spot[widest] + 1) % values.shape[widest]] + spot[widest + 1:]
    return values.at[tuple(spot)].set(least).at[tuple(beside)].set(largest)


def block_levels(own_key, dims, cuts, least, largest):
    level, own = 1.0, jax.random.fold_in(own_key, 6)
    for position, shards_of in cuts:
        steps = jnp.exp(jax.random.uniform(jax.random.fold_in(own, position), (shards_of,), jnp.float32, least / len(cuts), largest / len(cuts)))
        level = level * jnp.repeat(steps, dims[position] // shards_of).reshape([-1 if axis == position else 1 for axis in range(len(dims))])
    return level


def centred(rng, shape, width, most, shards=(), kind=jnp.bfloat16):
    array = jax.random.normal(rng, shape, jnp.float32) * width
    if len(shards) > 0:
        array = block_levels(rng, shape, shards, -0.22, 0.18) * array
    return jnp.clip(array, min=-most, max=most).astype(kind)


def setup_inputs(seed: int = 0) -> dict:
    splits = jax.random.split(jax.random.key(seed), 9)
    atm_fields = centred(splits[0], (NF, ATM_CELLS), 1.0, 6.0, ((1, 768),))
    ocn_fields = centred(splits[1], (NF, OCN_CELLS), 1.0, 6.0, ((1, 768),))
    transfer_scale = jnp.clip(jnp.exp(jax.random.uniform(splits[2], (NF,), jnp.float32, math.log(0.5), math.log(2.0))), 0.5, 2.0)
    atmosphere_slots = draw_atmosphere_slots(jax.random.fold_in(splits[8], 71), 0)
    ocn_slots = with_ends(jax.random.randint(splits[4], (BLOCKS, N_OCN, OCAP), 0, OCN_DEV), jax.random.fold_in(splits[4], 1), 0, OCN_DEV - 1).astype(jnp.int32)
    xc_ocean = draw_xc_ocean(jax.random.fold_in(splits[8], 71), 0)
    xc_area = jnp.clip(jnp.exp(math.log(1.0) - 1.6133518 * jax.random.uniform(splits[6], (BLOCKS, SLOTS), jnp.float32) ** block_levels(splits[6], (BLOCKS, SLOTS), ((0, 768),), -0.2, 0.2)), 0.19921875, 1.0).astype(jnp.bfloat16)
    xc_theta = jnp.clip(0.099609375 + 0.7988281 * jax.random.uniform(splits[7], (BLOCKS, SLOTS), jnp.float32) ** block_levels(splits[7], (BLOCKS, SLOTS), ((0, 768),), -0.2, 0.2), 0.099609375, 0.8984375).astype(jnp.bfloat16)
    return {"atm_fields": atm_fields, "ocn_fields": ocn_fields, "transfer_scale": transfer_scale, "atmosphere_slots": atmosphere_slots, "ocn_slots": ocn_slots, "xc_ocean": xc_ocean, "xc_area": xc_area, "xc_theta": xc_theta}


def surface_flux(air, sea, scale, area):
    a = air.astype(jnp.float32)
    s = sea.astype(jnp.float32)
    du = a[..., 1, :] - s[..., 1, :]
    dv = a[..., 2, :] - s[..., 2, :]
    speed = jnp.sqrt(du * du + dv * dv + 0.25)
    contrast = a[..., 0, :] - s[..., 0, :]
    coeff = jnp.ones_like(speed)
    for step in range(ITERS):
        coeff = 1.5 - 0.8 * jnp.tanh(0.3 * contrast * coeff / (speed * speed))
    return area * (scale[:, None] * (coeff * speed)[..., None, :] * (a - s))

def take_cols(table, index):
    return table[:, index]

def move_rows(values, partner):
    block_count = N_ATM * N_OCN
    spread = values.reshape(N_ATM, N_OCN, NF, SOURCE_BLOCKS, SLOT_CAPACITY).transpose(0, 1, 3, 2, 4)
    ocean_ids = jnp.arange(N_OCN, dtype=jnp.int32)
    row_ids = jnp.arange(SOURCE_BLOCKS, dtype=jnp.int32)
    picked_slots = spread[partner[:, None, :], ocean_ids[None, :, None], row_ids[None, None, :]]
    return picked_slots.transpose(0, 1, 3, 2, 4).reshape(block_count, NF, SOURCE_BLOCKS * SLOT_CAPACITY)

def reference(atm_fields, ocn_fields, transfer_scale, atmosphere_slots, ocn_slots, xc_ocean, xc_area, xc_theta):
    block_count = N_ATM * N_OCN
    slot_count = SOURCE_BLOCKS * SLOT_CAPACITY
    entry_count = N_OCN * OCAP
    atm_ids = jnp.arange(N_ATM, dtype=jnp.int32)
    row_ids = jnp.arange(SOURCE_BLOCKS, dtype=jnp.int32)
    source_of = (atm_ids[:, None] - row_ids[None, :] + RADIUS) % N_ATM
    target_of = (atm_ids[:, None] + row_ids[None, :] - RADIUS) % N_ATM
    atm_blocks = atm_fields.reshape(NF, block_count, ATM_DEV).transpose(1, 0, 2)
    atmosphere_index = atmosphere_slots.reshape(block_count, slot_count)
    atm_live = atmosphere_index >= 0
    atm_safe = jnp.maximum(atmosphere_index, 0)
    outgoing = jax.vmap(take_cols)(atm_blocks, atm_safe)
    outgoing = jnp.where(atm_live[:, None, :], outgoing, jnp.zeros((), jnp.bfloat16)).astype(jnp.bfloat16)
    air = move_rows(outgoing, source_of)
    ocn_blocks = ocn_fields.reshape(NF, block_count, OCN_DEV).transpose(1, 0, 2)
    sea_index = ocn_slots.reshape(block_count, entry_count)
    sea_out = jax.vmap(take_cols)(ocn_blocks, sea_index)
    entry_state = sea_out.reshape(N_ATM, N_OCN, NF, N_OCN, OCAP).transpose(0, 3, 2, 1, 4).reshape(block_count, NF, entry_count)
    first_owner = xc_ocean[:, 0, :]
    second_owner = xc_ocean[:, 1, :]
    live_mask = first_owner >= 0
    first_safe = jnp.maximum(first_owner, 0)
    second_safe = jnp.maximum(second_owner, 0)
    theta = xc_theta.astype(jnp.float32)
    first_vals = jax.vmap(take_cols)(entry_state, first_safe).astype(jnp.float32)
    second_vals = jax.vmap(take_cols)(entry_state, second_safe).astype(jnp.float32)
    sea = (theta[:, None, :] * first_vals + (1.0 - theta)[:, None, :] * second_vals).astype(jnp.bfloat16)
    flux = surface_flux(air, sea, transfer_scale, xc_area.astype(jnp.float32)[:, None, :])
    weighted = jnp.where(live_mask[:, None, :], flux, jnp.float32(0.0))
    back = move_rows(weighted, target_of)
    contrib = jnp.where(atm_live[:, None, :], back, jnp.float32(0.0))

    def add_atm(values, index):
        return jnp.zeros((NF, ATM_DEV), jnp.float32).at[:, index].add(values)
    atm_out = jax.vmap(add_atm)(contrib, atm_safe).transpose(1, 0, 2).reshape(NF, block_count * ATM_DEV)

    def add_entries(values, weight, index_one, index_two):
        total = jnp.zeros((NF, entry_count), jnp.float32)
        total = total.at[:, index_one].add(weight[None, :] * values)
        return total.at[:, index_two].add((1.0 - weight)[None, :] * values)
    entry_flux = jax.vmap(add_entries)(weighted, theta, first_safe, second_safe)
    returned = entry_flux.reshape(N_ATM, N_OCN, NF, N_OCN, OCAP).transpose(0, 3, 2, 1, 4).reshape(block_count, NF, entry_count)

    def add_ocean(values, index):
        return jnp.zeros((NF, OCN_DEV), jnp.float32).at[:, index].add(values)
    ocn_out = jax.vmap(add_ocean)(returned, sea_index).transpose(1, 0, 2).reshape(NF, block_count * OCN_DEV)
    return (atm_out, ocn_out)
```

```python
import functools
import jax
import jax.numpy as jnp
from jax import lax
from jax.experimental import pallas as pl
from jax.experimental.pallas import tpu as pltpu
from jax.sharding import Mesh, PartitionSpec as P

NF = 64
RADIUS = 3
CAP = 64
ITERS = 3
ROWS = 7
SLOTS = ROWS * CAP
W = 8
Y = 8
OCAP = 96
PAD = 128
EPAD = Y * PAD
ATM = 256
OCN = 384
MSG = NF + 16
BF = jnp.bfloat16
F32 = jnp.float32
VMEM = pl.BlockSpec(memory_space=pltpu.VMEM)
SMEM = pl.BlockSpec(memory_space=pltpu.SMEM)
NT = (((1,), (1,)), ((), ()))


def one_hot(rows, index):
    ids = lax.broadcasted_iota(jnp.int32, (rows, index.shape[1]), 0)
    return jnp.where(ids == index, 1.0, 0.0).astype(BF)


def entry_row(slots_ref, padded):
    padded[...] = jnp.full((Y, PAD), -1, jnp.int32)
    padded[:, :OCAP] = slots_ref[...]
    return jnp.concatenate([padded[o : o + 1, :] for o in range(Y)], axis=1)


def slot_row(slots_ref):
    return jnp.concatenate([slots_ref[k : k + 1, :] for k in range(ROWS)], axis=1)


def padded_entries(index):
    moved = index
    for o in range(1, Y):
        moved = moved + jnp.where(index >= o * OCAP, PAD - OCAP, 0)
    return moved


def flux(air, sea, scale, area, live):
    du = air[1:2] - sea[1:2]
    dv = air[2:3] - sea[2:3]
    square = du * du + dv * dv + 0.25
    speed = jnp.sqrt(square)
    contrast = air[0:1] - sea[0:1]
    coeff = jnp.ones_like(speed)
    for step in range(ITERS):
        coeff = 1.5 - 0.8 * jnp.tanh(0.3 * contrast * coeff / (speed * speed))
    factor = jnp.where(live, area * (coeff * speed), 0.0)
    return factor * (scale * (air - sea))


def halves(values):
    high = values.astype(BF)
    low = (values - high.astype(F32)).astype(BF)
    return jnp.concatenate([high, low], axis=0)


def summed_onto(values, picker):
    both = lax.dot_general(halves(values), picker, NT, preferred_element_type=F32)
    return both[:NF] + both[NF:]


def send_sea_kernel(fields_ref, slots_ref, out_ref, padded):
    picked = jnp.dot(
        fields_ref[...], one_hot(OCN, entry_row(slots_ref, padded)), preferred_element_type=F32
    ).astype(BF)
    for o in range(Y):
        out_ref[o] = picked[:, o * PAD : o * PAD + OCAP]


def send_air_kernel(place_ref, fields_ref, slots_ref, air_ref, own_ref, cross_ref):
    w = place_ref[0]
    picked = jnp.dot(
        fields_ref[...], one_hot(ATM, slot_row(slots_ref)), preferred_element_type=F32
    )
    air_ref[...] = picked.astype(BF)
    for k in range(ROWS):
        own_ref[lax.rem(w + (k - RADIUS + W), W)] = picked[:, k * CAP : (k + 1) * CAP].astype(BF)
    own_ref[lax.rem(w + W // 2, W)] = jnp.zeros((NF, CAP), BF)
    for j in range(RADIUS):
        cross_ref[j] = jnp.where(w >= W // 2, own_ref[j], own_ref[W - RADIUS + j])


def make_message_kernel(
    place_ref, entries_ref, ocean_ref, theta_ref, area_ref, own_ref, crossed_ref, sea_ref, msg_ref, table
):
    w = place_ref[0]
    table[...] = jnp.zeros((NF, EPAD), BF)
    for o in range(Y):
        table[:, o * PAD : o * PAD + OCAP] = entries_ref[o]
    index = padded_entries(ocean_ref[...])
    entries = table[...]
    first = jnp.dot(entries, one_hot(EPAD, index[0:1]), preferred_element_type=F32)
    second = jnp.dot(entries, one_hot(EPAD, index[1:2]), preferred_element_type=F32)
    theta = theta_ref[...].astype(F32)
    sea = theta * first + (1.0 - theta) * second
    sea_ref[...] = sea.astype(BF)
    area = jnp.broadcast_to(area_ref[...].astype(F32), (MSG - NF, SLOTS))
    both = jnp.concatenate([sea, area], axis=0)
    for p in range(W):
        mine = own_ref[p]
        if p < RADIUS:
            mine = jnp.where(w - p > W // 2, crossed_ref[p], mine)
        if p >= W - RADIUS:
            mine = jnp.where(p - w > W // 2, crossed_ref[p - (W - RADIUS)], mine)
        msg_ref[p, :NF, :CAP] = mine
        msg_ref[p, NF:, :CAP] = jnp.zeros((MSG - NF, CAP), BF)
    for k in range(ROWS):
        msg_ref[lax.rem(w + (RADIUS - k + W), W), :, CAP:] = both[:, k * CAP : (k + 1) * CAP].astype(BF)
    msg_ref[lax.rem(w + W // 2, W), :, CAP:] = jnp.zeros((MSG, CAP), BF)


def entry_flux_kernel(
    place_ref, got_ref, sea_ref, ocean_ref, theta_ref, area_ref, scale_ref, out_ref
):
    w = place_ref[0]
    air = jnp.concatenate(
        [got_ref[lax.rem(w + (RADIUS - k + W), W), :NF, :CAP].astype(F32) for k in range(ROWS)], axis=1
    )
    ocean = ocean_ref[...]
    weighted = flux(
        air, sea_ref[...].astype(F32), scale_ref[...], area_ref[...].astype(F32), ocean[0:1] >= 0
    )
    index = padded_entries(ocean)
    theta = theta_ref[...].astype(F32)
    total = summed_onto(theta * weighted, one_hot(EPAD, index[0:1]))
    total = total + summed_onto((1.0 - theta) * weighted, one_hot(EPAD, index[1:2]))
    total = total.astype(BF)
    for o in range(Y):
        out_ref[o] = total[:, o * PAD : o * PAD + OCAP]


def atm_flux_kernel(place_ref, got_ref, crossed_ref, air_ref, slots_ref, scale_ref, out_ref):
    w = place_ref[0]
    parts = []
    for k in range(ROWS):
        p = lax.rem(w + (k - RADIUS + W), W)
        here = got_ref[p, :, CAP:]
        there = jnp.where(p >= W - RADIUS, p - (W - RADIUS), jnp.minimum(p, RADIUS - 1))
        away = crossed_ref[there, :, CAP:]
        over = w + (k - RADIUS)
        parts.append(jnp.where((over < 0) | (over >= W), away, here).astype(F32))
    both = jnp.concatenate(parts, axis=1)
    index = slot_row(slots_ref)
    weighted = flux(
        air_ref[...].astype(F32), both[:NF], scale_ref[...], both[NF : NF + 1], index >= 0
    )
    out_ref[...] = summed_onto(weighted, one_hot(ATM, index))


def ocn_flux_kernel(got_ref, slots_ref, out_ref, padded, table):
    table[...] = jnp.zeros((NF, EPAD), BF)
    for o in range(Y):
        table[:, o * PAD : o * PAD + OCAP] = got_ref[o]
    picker = one_hot(OCN, entry_row(slots_ref, padded))
    out_ref[...] = lax.dot_general(table[...], picker, NT, preferred_element_type=F32)


def call(kernel, name, ins, outs, scratch=(), scalar=True):
    specs = [SMEM] + [VMEM] * (len(ins) - 1) if scalar else [VMEM] * len(ins)
    single = len(outs) == 1
    shapes = [jax.ShapeDtypeStruct(s, d) for s, d in outs]
    return pl.pallas_call(
        kernel,
        out_shape=shapes[0] if single else shapes,
        in_specs=specs,
        out_specs=VMEM if single else [VMEM] * len(outs),
        scratch_shapes=list(scratch),
        name=name,
        compiler_params=pltpu.CompilerParams(vmem_limit_bytes=24 * 1024 * 1024),
    )(*ins)


def on_device(
    planes, atm_fields, ocn_fields, transfer_scale, atmosphere_slots, ocn_slots, xc_ocean, xc_area, xc_theta
):
    w = lax.axis_index("w")
    place = w.reshape(1).astype(jnp.int32)
    atm_slots = atmosphere_slots[0]
    sea_slots = ocn_slots[0]
    ocean = xc_ocean[0]
    scale = transfer_scale[:, None]
    index_pad = pltpu.VMEM((Y, PAD), jnp.int32)
    table = pltpu.VMEM((NF, EPAD), BF)

    sending = call(
        send_sea_kernel, "send_sea", (ocn_fields, sea_slots), [((Y, NF, OCAP), BF)], [index_pad], scalar=False
    )
    entries = lax.all_to_all(sending, "ocn", 0, 0, tiled=True)

    air, own, cross = call(
        send_air_kernel,
        "send_air",
        (place, atm_fields, atm_slots),
        [((NF, SLOTS), BF), ((W, NF, CAP), BF), ((RADIUS, NF, CAP), BF)],
    )
    up, down = [], []
    for z in range(planes):
        for v in range(W):
            here, above, below = z * W + v, (z + 1) % planes * W + v, (z - 1) % planes * W + v
            if v >= W - RADIUS:
                up.append((here, above))
                down.append((here, below))
            if v < RADIUS:
                up.append((here, below))
                down.append((here, above))
    crossed = lax.ppermute(cross, ("z", "w"), up)

    sea, message = call(
        make_message_kernel,
        "make_message",
        (place, entries, ocean, xc_theta, xc_area, own, crossed),
        [((NF, SLOTS), BF), ((W, MSG, 2 * CAP), BF)],
        [table],
    )
    got = lax.all_to_all(message, "w", 0, 0, tiled=True)

    entry = call(
        entry_flux_kernel,
        "entry_flux",
        (place, got, sea, ocean, xc_theta, xc_area, scale),
        [((Y, NF, OCAP), BF)],
    )
    returned = lax.all_to_all(entry, "ocn", 0, 0, tiled=True)
    back = lax.ppermute(jnp.where(w < W // 2, got[W - RADIUS :], got[:RADIUS]), ("z", "w"), down)
    atm_flux = call(
        atm_flux_kernel,
        "atm_flux",
        (place, got, back, air, atm_slots, scale),
        [((NF, ATM), F32)],
    )
    ocn_flux = call(
        ocn_flux_kernel, "ocn_flux", (returned, sea_slots), [((NF, OCN), F32)], [index_pad, table], scalar=False
    )
    return (atm_flux, ocn_flux)


def solution(mesh):
    n_atm, n_ocn = mesh.shape["atm"], mesh.shape["ocn"]
    planes = n_atm // W
    split = Mesh(mesh.devices.reshape(planes, W, n_ocn), ("z", "w", "ocn"))
    every = ("z", "w", "ocn")
    placed = (
        P(None, every),
        P(None, every),
        P(),
        P(every, None, None),
        P(every, None, None),
        P(every, None, None),
        P(every, None),
        P(every, None),
    )
    return jax.shard_map(
        functools.partial(on_device, planes),
        mesh=split,
        in_specs=placed,
        out_specs=(P(None, every), P(None, every)),
        check_vma=False,
    )
```

```python
import functools
import jax
import jax.numpy as jnp
from jax import lax
from jax.experimental import pallas as pl
from jax.experimental.pallas import tpu as pltpu
from jax.sharding import Mesh, PartitionSpec as P

NF = 64
RADIUS = 3
CAP = 64
ITERS = 3
ROWS = 7
SLOTS = ROWS * CAP
W = 8
Y = 8
OCAP = 96
PAD = 128
EPAD = Y * PAD
ATM = 256
OCN = 384
MSG = NF + 16
BF = jnp.bfloat16
F32 = jnp.float32
VMEM = pl.BlockSpec(memory_space=pltpu.VMEM)
SMEM = pl.BlockSpec(memory_space=pltpu.SMEM)
NT = (((1,), (1,)), ((), ()))


def one_hot(rows, index):
    ids = lax.broadcasted_iota(jnp.int32, (rows, index.shape[1]), 0)
    return jnp.where(ids == index, 1.0, 0.0).astype(BF)


def padded_entries(index):
    moved = index
    for o in range(1, Y):
        moved = moved + jnp.where(index >= o * OCAP, PAD - OCAP, 0)
    return moved


def flux(air, sea, scale, area, live):
    du = air[1:2] - sea[1:2]
    dv = air[2:3] - sea[2:3]
    square = du * du + dv * dv + 0.25
    speed = jnp.sqrt(square)
    contrast = air[0:1] - sea[0:1]
    coeff = jnp.ones_like(speed)
    for step in range(ITERS):
        coeff = 1.5 - 0.8 * jnp.tanh(0.3 * contrast * coeff / (speed * speed))
    factor = jnp.where(live, area * (coeff * speed), 0.0)
    return factor * (scale * (air - sea))


def halves(values):
    high = values.astype(BF)
    low = (values - high.astype(F32)).astype(BF)
    return jnp.concatenate([high, low], axis=0)


def summed_onto(values, picker):
    both = lax.dot_general(halves(values), picker, NT, preferred_element_type=F32)
    return both[:NF] + both[NF:]


def send_kernel(
    place_ref, ocn_hbm, entries_hbm, atm_hbm, slots_hbm, ocean_hbm, theta_hbm, area_hbm, scale_hbm,
    out_ref, own_ref, cross_ref, air_ref, entry_row_ref, slot_row_ref, ocean_ref, theta_ref, area_ref, scale_ref,
    ocn_ref, entries_ref, atm_ref, slots_ref, row_ref, padded, sems,
):
    w = place_ref[0]
    pairs = [
        (entries_hbm, entries_ref),
        (ocn_hbm, ocn_ref),
        (slots_hbm, slots_ref),
        (atm_hbm, atm_ref),
        (ocean_hbm, ocean_ref),
        (theta_hbm, theta_ref),
        (area_hbm, area_ref),
        (scale_hbm, row_ref),
    ]
    copies = [pltpu.make_async_copy(a, b, sems.at[i]) for i, (a, b) in enumerate(pairs)]
    for copy in copies:
        copy.start()
    padded[...] = jnp.full((Y, PAD), -1, jnp.int32)
    copies[0].wait()
    padded[:, :OCAP] = entries_ref[...]
    index = jnp.concatenate([padded[o : o + 1, :] for o in range(Y)], axis=1)
    entry_row_ref[...] = index
    picker = one_hot(OCN, index)
    copies[1].wait()
    picked = jnp.dot(ocn_ref[...], picker, preferred_element_type=F32).astype(BF)
    for o in range(Y):
        out_ref[o] = picked[:, o * PAD : o * PAD + OCAP]
    copies[2].wait()
    index = jnp.concatenate([slots_ref[k] for k in range(ROWS)], axis=1)
    slot_row_ref[...] = index
    picker = one_hot(ATM, index)
    copies[3].wait()
    air = jnp.dot(atm_ref[...], picker, preferred_element_type=F32)
    air_ref[...] = air.astype(BF)
    for k in range(ROWS):
        own_ref[lax.rem(w + (k - RADIUS + W), W)] = air[:, k * CAP : (k + 1) * CAP].astype(BF)
    own_ref[lax.rem(w + W // 2, W)] = jnp.zeros((NF, CAP), BF)
    crossing = [jnp.where(w >= W // 2, own_ref[j], own_ref[W - RADIUS + j]).astype(F32) for j in range(RADIUS)]
    cross_ref[...] = jnp.concatenate(crossing, axis=1).astype(BF)
    for copy in copies[4:]:
        copy.wait()
    rows = lax.broadcasted_iota(jnp.int32, (NF, NF), 0)
    lanes = lax.broadcasted_iota(jnp.int32, (NF, NF), 1)
    scale_ref[...] = jnp.sum(jnp.where(rows == lanes, row_ref[...], 0.0), axis=1, keepdims=True)


def make_message_kernel(
    place_ref, entries_ref, ocean_ref, theta_ref, area_ref, own_ref, crossed_ref, sea_ref, msg_ref, table
):
    w = place_ref[0]
    table[...] = jnp.zeros((NF, EPAD), BF)
    for o in range(Y):
        table[:, o * PAD : o * PAD + OCAP] = entries_ref[o]
    index = padded_entries(ocean_ref[...])
    entries = table[...]
    first = jnp.dot(entries, one_hot(EPAD, index[0:1]), preferred_element_type=F32)
    second = jnp.dot(entries, one_hot(EPAD, index[1:2]), preferred_element_type=F32)
    theta = theta_ref[...].astype(F32)
    sea = theta * first + (1.0 - theta) * second
    sea_ref[...] = sea.astype(BF)
    area = jnp.broadcast_to(area_ref[...].astype(F32), (MSG - NF, SLOTS))
    both = jnp.concatenate([sea, area], axis=0)
    for p in range(W):
        mine = own_ref[p]
        if p < RADIUS or p >= W - RADIUS:
            j = p if p < RADIUS else p - (W - RADIUS)
            mine = jnp.where(jnp.abs(p - w) > W // 2, crossed_ref[:, j * CAP : (j + 1) * CAP], mine)
        msg_ref[p, :NF, :CAP] = mine
        msg_ref[p, NF:, :CAP] = jnp.zeros((MSG - NF, CAP), BF)
    for k in range(ROWS):
        msg_ref[lax.rem(w + (RADIUS - k + W), W), :, CAP:] = both[:, k * CAP : (k + 1) * CAP].astype(BF)
    msg_ref[lax.rem(w + W // 2, W), :, CAP:] = jnp.zeros((MSG, CAP), BF)


def entry_flux_kernel(
    place_ref, got_ref, sea_ref, ocean_ref, theta_ref, area_ref, scale_ref, out_ref, cross_ref
):
    w = place_ref[0]
    air = jnp.concatenate(
        [got_ref[lax.rem(w + (RADIUS - k + W), W), :NF, :CAP].astype(F32) for k in range(ROWS)], axis=1
    )
    ocean = ocean_ref[...]
    weighted = flux(
        air, sea_ref[...].astype(F32), scale_ref[...], area_ref[...].astype(F32), ocean[0:1] >= 0
    )
    index = padded_entries(ocean)
    theta = theta_ref[...].astype(F32)
    total = summed_onto(theta * weighted, one_hot(EPAD, index[0:1]))
    total = total + summed_onto((1.0 - theta) * weighted, one_hot(EPAD, index[1:2]))
    total = total.astype(BF)
    for o in range(Y):
        out_ref[o] = total[:, o * PAD : o * PAD + OCAP]
    first = jnp.where(w < W // 2, W - RADIUS, 0)
    crossing = [got_ref[first + j, :, CAP:].astype(F32) for j in range(RADIUS)]
    cross_ref[...] = jnp.concatenate(crossing, axis=1).astype(BF)


def atm_flux_kernel(place_ref, got_ref, crossed_ref, air_ref, slots_ref, scale_ref, out_ref, spread):
    w = place_ref[0]
    for p in range(W):
        here = got_ref[p, :, CAP:]
        if p < RADIUS or p >= W - RADIUS:
            j = p if p < RADIUS else p - (W - RADIUS)
            here = jnp.where(jnp.abs(p - w) > W // 2, crossed_ref[:, j * CAP : (j + 1) * CAP], here)
        spread[p] = here.astype(F32)
    both = jnp.concatenate([spread[lax.rem(w + (k - RADIUS + W), W)] for k in range(ROWS)], axis=1)
    index = slots_ref[...]
    weighted = flux(
        air_ref[...].astype(F32), both[:NF], scale_ref[...], both[NF : NF + 1], index >= 0
    )
    out_ref[...] = summed_onto(weighted, one_hot(ATM, index))


def ocn_flux_kernel(place_ref, returned_ref, entries_ref, out_ref, table):
    table[...] = jnp.zeros((NF, EPAD), BF)
    for o in range(Y):
        table[:, o * PAD : o * PAD + OCAP] = returned_ref[o]
    picker = one_hot(OCN, entries_ref[...])
    out_ref[...] = lax.dot_general(table[...], picker, NT, preferred_element_type=F32)


def call(kernel, name, ins, outs, scratch=(), space=pltpu.VMEM):
    specs = [SMEM] + [pl.BlockSpec(memory_space=space)] * (len(ins) - 1)
    single = len(outs) == 1
    shapes = [jax.ShapeDtypeStruct(s, d) for s, d in outs]
    return pl.pallas_call(
        kernel,
        out_shape=shapes[0] if single else shapes,
        in_specs=specs,
        out_specs=VMEM if single else [VMEM] * len(outs),
        scratch_shapes=list(scratch),
        name=name,
        compiler_params=pltpu.CompilerParams(vmem_limit_bytes=24 * 1024 * 1024),
    )(*ins)


def on_device(
    planes, atm_fields, ocn_fields, transfer_scale, atmosphere_slots, ocn_slots, xc_ocean, xc_area, xc_theta
):
    w = lax.axis_index("w")
    place = w.reshape(1).astype(jnp.int32)
    table = pltpu.VMEM((NF, EPAD), BF)
    given = (
        ocn_fields,
        ocn_slots[0],
        atm_fields,
        atmosphere_slots.reshape(ROWS, 1, CAP),
        xc_ocean[0],
        xc_theta,
        xc_area,
        transfer_scale[None, :],
    )
    sending, own, cross, air, entry_row, slot_row, ocean, theta, area, scale = call(
        send_kernel,
        "send",
        (place, *(pltpu.with_memory_space_constraint(x, pltpu.HBM) for x in given)),
        [
            ((Y, NF, OCAP), BF),
            ((W, NF, CAP), BF),
            ((NF, RADIUS * CAP), BF),
            ((NF, SLOTS), BF),
            ((1, EPAD), jnp.int32),
            ((1, SLOTS), jnp.int32),
            ((2, SLOTS), jnp.int32),
            ((1, SLOTS), BF),
            ((1, SLOTS), BF),
            ((NF, 1), F32),
        ],
        [
            pltpu.VMEM((NF, OCN), BF),
            pltpu.VMEM((Y, OCAP), jnp.int32),
            pltpu.VMEM((NF, ATM), BF),
            pltpu.VMEM((ROWS, 1, CAP), jnp.int32),
            pltpu.VMEM((1, NF), F32),
            pltpu.VMEM((Y, PAD), jnp.int32),
            pltpu.SemaphoreType.DMA((8,)),
        ],
        pltpu.HBM,
    )
    up, down = [], []
    for z in range(planes):
        for v in range(W):
            here, above, below = z * W + v, (z + 1) % planes * W + v, (z - 1) % planes * W + v
            if v >= W - RADIUS:
                up.append((here, above))
                down.append((here, below))
            if v < RADIUS:
                up.append((here, below))
                down.append((here, above))
    entries = lax.all_to_all(sending, "ocn", 0, 0, tiled=True)
    crossed = lax.ppermute(cross, ("z", "w"), up)
    sea, message = call(
        make_message_kernel,
        "make_message",
        (place, entries, ocean, theta, area, own, crossed),
        [((NF, SLOTS), BF), ((W, MSG, 2 * CAP), BF)],
        [table],
    )
    got = lax.all_to_all(message, "w", 0, 0, tiled=True)
    entry, away = call(
        entry_flux_kernel,
        "entry_flux",
        (place, got, sea, ocean, theta, area, scale),
        [((Y, NF, OCAP), BF), ((MSG, RADIUS * CAP), BF)],
    )
    returned = lax.all_to_all(entry, "ocn", 0, 0, tiled=True)
    back = lax.ppermute(away, ("z", "w"), down)
    atm_flux = call(
        atm_flux_kernel,
        "atm_flux",
        (place, got, back, air, slot_row, scale),
        [((NF, ATM), F32)],
        [pltpu.VMEM((W, MSG, CAP), F32)],
    )
    ocn_flux = call(ocn_flux_kernel, "ocn_flux", (place, returned, entry_row), [((NF, OCN), F32)], [table])
    return (atm_flux, ocn_flux)


def solution(mesh):
    n_atm, n_ocn = mesh.shape["atm"], mesh.shape["ocn"]
    planes = n_atm // W
    split = Mesh(mesh.devices.reshape(planes, W, n_ocn), ("z", "w", "ocn"))
    every = ("z", "w", "ocn")
    placed = (
        P(None, every),
        P(None, every),
        P(),
        P(every, None, None),
        P(every, None, None),
        P(every, None, None),
        P(every, None),
        P(every, None),
    )
    return jax.shard_map(
        functools.partial(on_device, planes),
        mesh=split,
        in_specs=placed,
        out_specs=(P(None, every), P(None, every)),
        check_vma=False,
    )
```

```python
import functools
import jax
import jax.numpy as jnp
from jax import lax
from jax.experimental import pallas as pl
from jax.experimental.pallas import tpu as pltpu
from jax.sharding import Mesh, PartitionSpec as P

NF = 64
RADIUS = 3
CAP = 64
ITERS = 3
ROWS = 7
SLOTS = ROWS * CAP
W = 8
Y = 8
OCAP = 96
PAD = 128
EPAD = Y * PAD
ATM = 256
OCN = 384
MSG = NF + 16
PIECES = 2
WIDE = 1536
BF = jnp.bfloat16
F32 = jnp.float32
VMEM = pl.BlockSpec(memory_space=pltpu.VMEM)
SMEM = pl.BlockSpec(memory_space=pltpu.SMEM)
NT = (((1,), (1,)), ((), ()))


def one_hot(rows, index):
    ids = lax.broadcasted_iota(jnp.int32, (rows, index.shape[1]), 0)
    return jnp.where(ids == index, 1.0, 0.0).astype(BF)


def padded_entries(index):
    moved = index
    for o in range(1, Y):
        moved = moved + jnp.where(index >= o * OCAP, PAD - OCAP, 0)
    return moved


def flux(air, sea, scale, area, live):
    du = air[1:2] - sea[1:2]
    dv = air[2:3] - sea[2:3]
    square = du * du + dv * dv + 0.25
    speed = jnp.sqrt(square)
    contrast = air[0:1] - sea[0:1]
    coeff = jnp.ones_like(speed)
    for step in range(ITERS):
        coeff = 1.5 - 0.8 * jnp.tanh(0.3 * contrast * coeff / (speed * speed))
    factor = jnp.where(live, area * (coeff * speed), 0.0)
    return factor * (scale * (air - sea))


def halves(values):
    high = values.astype(BF)
    low = (values - high.astype(F32)).astype(BF)
    return jnp.concatenate([high, low], axis=0)


def summed_onto(values, picker):
    both = lax.dot_general(values, picker, NT, preferred_element_type=F32)
    return both[:NF] + both[NF:]


def send_kernel(
    place_ref, ocn_hbm, entries_hbm, atm_hbm, slots_hbm, ocean_hbm, theta_hbm, area_hbm, scale_hbm,
    out_hbm, own_ref, cross_ref, wide_ref, air_ref, entry_row_ref, slot_row_ref, ocean_ref, theta_ref, area_ref, scale_ref,
    ocn_ref, entries_ref, atm_ref, slots_ref, row_ref, padded, placed, out_ref, sems,
):
    w = place_ref[0]
    pairs = [
        (entries_hbm, entries_ref),
        (ocn_hbm, ocn_ref),
        (slots_hbm, slots_ref),
        (atm_hbm, atm_ref),
        (ocean_hbm, ocean_ref),
        (theta_hbm, theta_ref),
        (area_hbm, area_ref),
        (scale_hbm, row_ref),
    ]
    copies = [pltpu.make_async_copy(a, b, sems.at[i]) for i, (a, b) in enumerate(pairs)]
    for copy in copies:
        copy.start()
    padded[...] = jnp.full((Y, PAD), -1, jnp.int32)
    copies[0].wait()
    padded[:, :OCAP] = entries_ref[...]
    index = jnp.concatenate([padded[o : o + 1, :] for o in range(Y)], axis=1)
    entry_row_ref[...] = index
    picker = one_hot(OCN, index)
    copies[1].wait()
    picked = jnp.dot(ocn_ref[...], picker, preferred_element_type=F32).astype(BF)
    for o in range(Y):
        out_ref[o] = picked[:, o * PAD : o * PAD + OCAP]
    leave = pltpu.make_async_copy(out_ref, out_hbm, sems.at[len(pairs)])
    leave.start()
    copies[2].wait()
    for k in range(ROWS):
        placed[lax.rem(w + (k - RADIUS + W), W)] = slots_ref[k]
    placed[lax.rem(w + W // 2, W)] = jnp.full((1, CAP), -1, jnp.int32)
    index = jnp.concatenate([placed[p] for p in range(W)], axis=1)
    slot_row_ref[...] = index
    picker = one_hot(ATM, index)
    copies[3].wait()
    air = jnp.dot(atm_ref[...], picker, preferred_element_type=F32)
    crossing = jnp.where(w >= W // 2, air[:, : RADIUS * CAP], air[:, (W - RADIUS) * CAP :]).astype(BF)
    cross_ref[...] = crossing
    wide_ref[...] = jnp.zeros((NF, WIDE), BF)
    wide_ref[:, : RADIUS * CAP] = crossing
    air_ref[...] = air.astype(BF)
    for p in range(W):
        own_ref[p] = air[:, p * CAP : (p + 1) * CAP].astype(BF)
    for copy in copies[4:]:
        copy.wait()
    rows = lax.broadcasted_iota(jnp.int32, (NF, NF), 0)
    lanes = lax.broadcasted_iota(jnp.int32, (NF, NF), 1)
    scale_ref[...] = jnp.sum(jnp.where(rows == lanes, row_ref[...], 0.0), axis=1, keepdims=True)
    leave.wait()


def make_message_kernel(
    place_ref, entries_ref, ocean_ref, theta_ref, area_ref, own_ref, up_ref, down_ref, sea_ref, msg_ref, table
):
    w = place_ref[0]
    table[...] = jnp.zeros((NF, EPAD), BF)
    for o in range(Y):
        table[:, o * PAD : o * PAD + OCAP] = entries_ref[o]
    index = padded_entries(ocean_ref[...])
    entries = table[...]
    first = jnp.dot(entries, one_hot(EPAD, index[0:1]), preferred_element_type=F32)
    second = jnp.dot(entries, one_hot(EPAD, index[1:2]), preferred_element_type=F32)
    theta = theta_ref[...].astype(F32)
    sea = theta * first + (1.0 - theta) * second
    sea_ref[...] = sea.astype(BF)
    area = jnp.broadcast_to(area_ref[...].astype(F32), (MSG - NF, SLOTS))
    both = jnp.concatenate([sea, area], axis=0)
    for p in range(W):
        mine = own_ref[p]
        if p < RADIUS or p >= W - RADIUS:
            j = p if p < RADIUS else p - (W - RADIUS)
            there = up_ref if p < RADIUS else down_ref
            mine = jnp.where(jnp.abs(p - w) > W // 2, there[:, j * CAP : (j + 1) * CAP], mine)
        msg_ref[p, :NF, :CAP] = mine
        msg_ref[p, NF:, :CAP] = jnp.zeros((MSG - NF, CAP), BF)
    for k in range(ROWS):
        msg_ref[lax.rem(w + (RADIUS - k + W), W), :, CAP:] = both[:, k * CAP : (k + 1) * CAP].astype(BF)
    msg_ref[lax.rem(w + W // 2, W), :, CAP:] = jnp.zeros((MSG, CAP), BF)


def entry_flux_kernel(
    place_ref, got_ref, sea_ref, ocean_ref, theta_ref, area_ref, scale_ref, out_hbm, cross_ref, out_ref, sems
):
    w = place_ref[0]
    air = jnp.concatenate(
        [got_ref[lax.rem(w + (RADIUS - k + W), W), :NF, :CAP].astype(F32) for k in range(ROWS)], axis=1
    )
    ocean = ocean_ref[...]
    weighted = flux(
        air, sea_ref[...].astype(F32), scale_ref[...], area_ref[...].astype(F32), ocean[0:1] >= 0
    )
    index = padded_entries(ocean)
    theta = theta_ref[...].astype(F32)
    one = halves(theta * weighted)
    two = halves((1.0 - theta) * weighted)
    part = Y // PIECES
    copies = []
    for i in range(PIECES):
        start = i * part * PAD
        total = summed_onto(one, one_hot(part * PAD, index[0:1] - start))
        total = total + summed_onto(two, one_hot(part * PAD, index[1:2] - start))
        total = total.astype(BF)
        for o in range(part):
            out_ref[i * part + o] = total[:, o * PAD : o * PAD + OCAP]
        rows = pl.ds(i * part, part)
        copy = pltpu.make_async_copy(out_ref.at[rows], out_hbm.at[rows], sems.at[i])
        copy.start()
        copies.append(copy)
    first = jnp.where(w < W // 2, W - RADIUS, 0)
    crossing = [got_ref[first + j, :, CAP:].astype(F32) for j in range(RADIUS)]
    cross_ref[...] = jnp.concatenate(crossing, axis=1).astype(BF)
    for copy in copies:
        copy.wait()


def near_flux_kernel(place_ref, got_ref, air_ref, slots_ref, scale_ref, out_ref):
    w = place_ref[0]
    both = jnp.concatenate([got_ref[p, :, CAP:].astype(F32) for p in range(W)], axis=1)
    slots = slots_ref[...]
    index = jnp.concatenate(
        [jnp.where(jnp.abs(p - w) > W // 2, -1, slots[:, p * CAP : (p + 1) * CAP]) for p in range(W)], axis=1
    )
    weighted = flux(
        air_ref[...].astype(F32), both[:NF], scale_ref[...], both[NF : NF + 1], index >= 0
    )
    out_ref[...] = summed_onto(halves(weighted), one_hot(ATM, index))


def last_kernel(
    place_ref, returned_ref, entries_ref, near_ref, crossed_ref, air_ref, slots_ref, scale_ref,
    atm_hbm, ocn_hbm, atm_ref, ocn_ref, table, sems,
):
    w = place_ref[0]
    table[...] = jnp.zeros((NF, EPAD), BF)
    for o in range(Y):
        table[:, o * PAD : o * PAD + OCAP] = returned_ref[o]
    picker = one_hot(OCN, entries_ref[...])
    ocn_ref[...] = lax.dot_general(table[...], picker, NT, preferred_element_type=F32)
    ocn_copy = pltpu.make_async_copy(ocn_ref, ocn_hbm, sems.at[0])
    ocn_copy.start()
    low = w >= W // 2
    count = RADIUS * CAP
    last = (W - RADIUS) * CAP
    air = jnp.where(low, air_ref[:, :count].astype(F32), air_ref[:, last:].astype(F32))
    slots = jnp.where(low, slots_ref[:, :count], slots_ref[:, last:])
    first = jnp.where(low, 0, W - RADIUS)
    index = jnp.concatenate(
        [
            jnp.where(jnp.abs(first + j - w) > W // 2, slots[:, j * CAP : (j + 1) * CAP], -1)
            for j in range(RADIUS)
        ],
        axis=1,
    )
    both = crossed_ref[...].astype(F32)
    weighted = flux(air, both[:NF], scale_ref[...], both[NF : NF + 1], index >= 0)
    atm_ref[...] = near_ref[...] + summed_onto(halves(weighted), one_hot(ATM, index))
    atm_copy = pltpu.make_async_copy(atm_ref, atm_hbm, sems.at[1])
    atm_copy.start()
    ocn_copy.wait()
    atm_copy.wait()


def call(kernel, name, ins, outs, scratch=(), space=pltpu.VMEM, first=pltpu.VMEM, rest=pltpu.VMEM):
    specs = [SMEM] + [pl.BlockSpec(memory_space=space)] * (len(ins) - 1)
    single = len(outs) == 1
    shapes = [jax.ShapeDtypeStruct(s, d) for s, d in outs]
    return pl.pallas_call(
        kernel,
        out_shape=shapes[0] if single else shapes,
        in_specs=specs,
        out_specs=pl.BlockSpec(memory_space=first) if single else [pl.BlockSpec(memory_space=x) for x in [first] + [rest] * (len(outs) - 1)],
        scratch_shapes=list(scratch),
        name=name,
        compiler_params=pltpu.CompilerParams(vmem_limit_bytes=24 * 1024 * 1024),
    )(*ins)


def on_device(
    planes, atm_fields, ocn_fields, transfer_scale, atmosphere_slots, ocn_slots, xc_ocean, xc_area, xc_theta
):
    w = lax.axis_index("w")
    place = w.reshape(1).astype(jnp.int32)
    table = pltpu.VMEM((NF, EPAD), BF)
    given = (
        ocn_fields,
        ocn_slots[0],
        atm_fields,
        atmosphere_slots.reshape(ROWS, 1, CAP),
        xc_ocean[0],
        xc_theta,
        xc_area,
        transfer_scale[None, :],
    )
    sending, own, cross, wide, air, entry_row, slot_row, ocean, theta, area, scale = call(
        send_kernel,
        "send",
        (place, *(pltpu.with_memory_space_constraint(x, pltpu.HBM) for x in given)),
        [
            ((Y, NF, OCAP), BF),
            ((W, NF, CAP), BF),
            ((NF, RADIUS * CAP), BF),
            ((NF, WIDE), BF),
            ((NF, W * CAP), BF),
            ((1, EPAD), jnp.int32),
            ((1, W * CAP), jnp.int32),
            ((2, SLOTS), jnp.int32),
            ((1, SLOTS), BF),
            ((1, SLOTS), BF),
            ((NF, 1), F32),
        ],
        [
            pltpu.VMEM((NF, OCN), BF),
            pltpu.VMEM((Y, OCAP), jnp.int32),
            pltpu.VMEM((NF, ATM), BF),
            pltpu.VMEM((ROWS, 1, CAP), jnp.int32),
            pltpu.VMEM((1, NF), F32),
            pltpu.VMEM((Y, PAD), jnp.int32),
            pltpu.VMEM((W, 1, CAP), jnp.int32),
            pltpu.VMEM((Y, NF, OCAP), BF),
            pltpu.SemaphoreType.DMA((9,)),
        ],
        pltpu.HBM,
        pltpu.HBM,
    )
    up, down = [], []
    for z in range(planes):
        for v in range(W):
            here, above, below = z * W + v, (z + 1) % planes * W + v, (z - 1) % planes * W + v
            if v >= W - RADIUS:
                up.append((here, above))
                down.append((here, below))
            if v < RADIUS:
                up.append((here, below))
                down.append((here, above))
    entries = lax.all_to_all(sending, "ocn", 0, 0, tiled=True)
    rising = [pair for pair in up if pair[0] % W >= W // 2]
    falling = [pair for pair in up if pair[0] % W < W // 2]
    crossed_up = lax.ppermute(wide, ("z", "w"), rising)
    crossed_down = lax.ppermute(cross, ("z", "w"), falling)
    sea, message = call(
        make_message_kernel,
        "make_message",
        (place, entries, ocean, theta, area, own, crossed_up, crossed_down),
        [((NF, SLOTS), BF), ((W, MSG, 2 * CAP), BF)],
        [table],
    )
    got = lax.all_to_all(message, "w", 0, 0, tiled=True)
    entry, away = call(
        entry_flux_kernel,
        "entry_flux",
        (place, got, sea, ocean, theta, area, scale),
        [((Y, NF, OCAP), BF), ((MSG, RADIUS * CAP), BF)],
        [pltpu.VMEM((Y, NF, OCAP), BF), pltpu.SemaphoreType.DMA((PIECES,))],
        first=pltpu.HBM,
    )
    returned = lax.all_to_all(entry, "ocn", 0, 0, tiled=True)
    back = lax.ppermute(away, ("z", "w"), down)
    near = call(near_flux_kernel, "near_flux", (place, got, air, slot_row, scale), [((NF, ATM), F32)])
    return call(
        last_kernel,
        "last",
        (place, returned, entry_row, near, back, air, slot_row, scale),
        [((NF, ATM), F32), ((NF, OCN), F32)],
        [pltpu.VMEM((NF, ATM), F32), pltpu.VMEM((NF, OCN), F32), table, pltpu.SemaphoreType.DMA((2,))],
        first=pltpu.HBM,
        rest=pltpu.HBM,
    )


def solution(mesh):
    n_atm, n_ocn = mesh.shape["atm"], mesh.shape["ocn"]
    planes = n_atm // W
    split = Mesh(mesh.devices.reshape(planes, W, n_ocn), ("z", "w", "ocn"))
    every = ("z", "w", "ocn")
    placed = (
        P(None, every),
        P(None, every),
        P(),
        P(every, None, None),
        P(every, None, None),
        P(every, None, None),
        P(every, None),
        P(every, None),
    )
    return jax.shard_map(
        functools.partial(on_device, planes),
        mesh=split,
        in_specs=placed,
        out_specs=(P(None, every), P(None, every)),
        check_vma=False,
    )
```

```python
import functools
import jax
import jax.numpy as jnp
from jax import lax
from jax.experimental import pallas as pl
from jax.experimental.pallas import tpu as pltpu
from jax.sharding import Mesh, PartitionSpec as P

NF = 64
RADIUS = 3
CAP = 64
ITERS = 3
ROWS = 7
SLOTS = ROWS * CAP
W = 8
Y = 8
OCAP = 96
PAD = 128
EPAD = Y * PAD
ATM = 256
OCN = 384
MSG = NF + 16
WIDE = 1536
BF = jnp.bfloat16
F32 = jnp.float32
VMEM = pl.BlockSpec(memory_space=pltpu.VMEM)
SMEM = pl.BlockSpec(memory_space=pltpu.SMEM)


def one_hot(rows, index):
    ids = lax.broadcasted_iota(jnp.int32, (rows, index.shape[1]), 0)
    return jnp.where(ids == index, 1.0, 0.0).astype(BF)


def padded_entries(index):
    moved = index
    for o in range(1, Y):
        moved = moved + jnp.where(index >= o * OCAP, PAD - OCAP, 0)
    return moved


def flux(air, sea, scale, area, live):
    du = air[1:2] - sea[1:2]
    dv = air[2:3] - sea[2:3]
    square = du * du + dv * dv + 0.25
    speed = jnp.sqrt(square)
    contrast = air[0:1] - sea[0:1]
    coeff = jnp.ones_like(speed)
    for step in range(ITERS):
        coeff = 1.5 - 0.8 * jnp.tanh(0.3 * contrast * coeff / (speed * speed))
    factor = jnp.where(live, area * (coeff * speed), 0.0)
    return factor * (scale * (air - sea))


def halves(values):
    high = values.astype(BF)
    low = (values - high.astype(F32)).astype(BF)
    return jnp.concatenate([high, low], axis=0)


def one_hot_rows(index, columns):
    ids = lax.broadcasted_iota(jnp.int32, (index.shape[0], columns), 1)
    return jnp.where(ids == index, 1.0, 0.0).astype(BF)


def summed_onto(values, picker):
    both = jnp.dot(values, picker, preferred_element_type=F32)
    return both[:NF] + both[NF:]


def send_kernel(
    place_ref, ocn_hbm, entries_hbm, atm_hbm, slots_hbm, ocean_hbm, theta_hbm, area_hbm, scale_hbm,
    out_hbm, own_ref, cross_ref, wide_ref, air_ref, entry_row_ref, slot_row_ref, ocean_ref, theta_ref, area_ref, scale_ref,
    ocn_ref, entries_ref, atm_ref, slots_ref, row_ref, padded, placed, out_ref, sems,
):
    w = place_ref[0]
    pairs = [
        (entries_hbm, entries_ref),
        (ocn_hbm, ocn_ref),
        (slots_hbm, slots_ref),
        (atm_hbm, atm_ref),
        (ocean_hbm, ocean_ref),
        (theta_hbm, theta_ref),
        (area_hbm, area_ref),
        (scale_hbm, row_ref),
    ]
    copies = [pltpu.make_async_copy(a, b, sems.at[i]) for i, (a, b) in enumerate(pairs)]
    for copy in copies:
        copy.start()
    padded[...] = jnp.full((Y, PAD), -1, jnp.int32)
    copies[0].wait()
    padded[:, :OCAP] = entries_ref[...]
    index = jnp.concatenate([padded[o : o + 1, :] for o in range(Y)], axis=1)
    entry_row_ref[...] = index
    picker = one_hot(OCN, index)
    copies[1].wait()
    picked = jnp.dot(ocn_ref[...], picker, preferred_element_type=F32).astype(BF)
    for o in range(Y):
        out_ref[o] = picked[:, o * PAD : o * PAD + OCAP]
    leave = pltpu.make_async_copy(out_ref, out_hbm, sems.at[len(pairs)])
    leave.start()
    copies[2].wait()
    for k in range(ROWS):
        placed[lax.rem(w + (k - RADIUS + W), W)] = slots_ref[k]
    placed[lax.rem(w + W // 2, W)] = jnp.full((1, CAP), -1, jnp.int32)
    index = jnp.concatenate([placed[p] for p in range(W)], axis=1)
    slot_row_ref[...] = index
    picker = one_hot(ATM, index)
    copies[3].wait()
    air = jnp.dot(atm_ref[...], picker, preferred_element_type=F32)
    crossing = jnp.where(w >= W // 2, air[:, : RADIUS * CAP], air[:, (W - RADIUS) * CAP :]).astype(BF)
    cross_ref[...] = crossing
    wide_ref[...] = jnp.zeros((NF, WIDE), BF)
    wide_ref[:, : RADIUS * CAP] = crossing
    air_ref[...] = air.astype(BF)
    for p in range(W):
        own_ref[p] = air[:, p * CAP : (p + 1) * CAP].astype(BF)
    for copy in copies[4:]:
        copy.wait()
    rows = lax.broadcasted_iota(jnp.int32, (NF, NF), 0)
    lanes = lax.broadcasted_iota(jnp.int32, (NF, NF), 1)
    scale_ref[...] = jnp.sum(jnp.where(rows == lanes, row_ref[...], 0.0), axis=1, keepdims=True)
    leave.wait()


def columns_kernel(place_ref, entries_ref, slots_ref, ocean_ref, out_ref, rows_ref):
    rows_ref[...] = jnp.full((8, EPAD), -1, jnp.int32)
    rows_ref[0:1] = entries_ref[...]
    rows_ref[1:2, : W * CAP] = slots_ref[...]
    rows_ref[2:4, :SLOTS] = padded_entries(ocean_ref[...])
    out_ref[...] = rows_ref[...].T


def make_message_kernel(
    place_ref, entries_ref, ocean_ref, theta_ref, area_ref, own_ref, cols_ref, sea_ref, msg_ref, table
):
    w = place_ref[0]
    table[...] = jnp.zeros((NF, EPAD), BF)
    for o in range(Y):
        table[:, o * PAD : o * PAD + OCAP] = entries_ref[o]
    index = padded_entries(ocean_ref[...])
    entries = table[...]
    first = jnp.dot(entries, one_hot(EPAD, index[0:1]), preferred_element_type=F32)
    second = jnp.dot(entries, one_hot(EPAD, index[1:2]), preferred_element_type=F32)
    theta = theta_ref[...].astype(F32)
    sea = theta * first + (1.0 - theta) * second
    sea_ref[...] = sea.astype(BF)
    area = jnp.broadcast_to(area_ref[...].astype(F32), (MSG - NF, SLOTS))
    both = jnp.concatenate([sea, area], axis=0)
    for p in range(W):
        msg_ref[p, :NF, :CAP] = own_ref[p]
        msg_ref[p, NF:, :CAP] = jnp.zeros((MSG - NF, CAP), BF)
    for k in range(ROWS):
        msg_ref[lax.rem(w + (RADIUS - k + W), W), :, CAP:] = both[:, k * CAP : (k + 1) * CAP].astype(BF)
    msg_ref[lax.rem(w + W // 2, W), :, CAP:] = jnp.zeros((MSG, CAP), BF)


def add_crossed_kernel(place_ref, msg_ref, up_ref, down_ref, out_ref):
    w = place_ref[0]
    for p in range(W):
        out_ref[p] = msg_ref[p]
        if p < RADIUS or p >= W - RADIUS:
            j = p if p < RADIUS else p - (W - RADIUS)
            there = up_ref if p < RADIUS else down_ref
            mine = msg_ref[p, :NF, :CAP]
            mine = jnp.where(jnp.abs(p - w) > W // 2, there[:, j * CAP : (j + 1) * CAP], mine)
            out_ref[p, :NF, :CAP] = mine


def entry_flux_kernel(
    place_ref, got_ref, sea_ref, ocean_ref, theta_ref, area_ref, scale_ref, cols_ref, out_ref, cross_ref
):
    w = place_ref[0]
    air = jnp.concatenate(
        [got_ref[lax.rem(w + (RADIUS - k + W), W), :NF, :CAP].astype(F32) for k in range(ROWS)], axis=1
    )
    weighted = flux(
        air, sea_ref[...].astype(F32), scale_ref[...], area_ref[...].astype(F32), ocean_ref[0:1, :] >= 0
    )
    theta = theta_ref[...].astype(F32)
    total = summed_onto(halves(theta * weighted), one_hot_rows(cols_ref[:SLOTS, 2:3], EPAD))
    total = total + summed_onto(halves((1.0 - theta) * weighted), one_hot_rows(cols_ref[:SLOTS, 3:4], EPAD))
    total = total.astype(BF)
    for o in range(Y):
        out_ref[o] = total[:, o * PAD : o * PAD + OCAP]
    first = jnp.where(w < W // 2, W - RADIUS, 0)
    crossing = [got_ref[first + j, :, CAP:].astype(F32) for j in range(RADIUS)]
    cross_ref[...] = jnp.concatenate(crossing, axis=1).astype(BF)


def near_flux_kernel(place_ref, got_ref, air_ref, slots_ref, scale_ref, cols_ref, out_ref):
    w = place_ref[0]
    both = jnp.concatenate([got_ref[p, :, CAP:].astype(F32) for p in range(W)], axis=1)
    slots = slots_ref[...]
    index = jnp.concatenate(
        [jnp.where(jnp.abs(p - w) > W // 2, -1, slots[:, p * CAP : (p + 1) * CAP]) for p in range(W)], axis=1
    )
    weighted = flux(
        air_ref[...].astype(F32), both[:NF], scale_ref[...], both[NF : NF + 1], index >= 0
    )
    out_ref[...] = summed_onto(halves(weighted), one_hot_rows(cols_ref[: W * CAP, 1:2], ATM))


def ocn_flux_kernel(place_ref, returned_ref, cols_ref, out_ref, table):
    table[...] = jnp.zeros((NF, EPAD), BF)
    for o in range(Y):
        table[:, o * PAD : o * PAD + OCAP] = returned_ref[o]
    out_ref[...] = jnp.dot(table[...], one_hot_rows(cols_ref[:, 0:1], OCN), preferred_element_type=F32)


def last_kernel(
    place_ref, ocn_ref, near_ref, crossed_ref, air_ref, slots_ref, scale_ref, cols_ref,
    atm_hbm, ocn_hbm, atm_ref, sems,
):
    w = place_ref[0]
    ocn_copy = pltpu.make_async_copy(ocn_ref, ocn_hbm, sems.at[0])
    ocn_copy.start()
    low = w >= W // 2
    count = RADIUS * CAP
    last = (W - RADIUS) * CAP
    air = jnp.where(low, air_ref[:, :count].astype(F32), air_ref[:, last:].astype(F32))
    slots = jnp.where(low, slots_ref[:, :count], slots_ref[:, last:])
    first = jnp.where(low, 0, W - RADIUS)
    index = jnp.concatenate(
        [
            jnp.where(jnp.abs(first + j - w) > W // 2, slots[:, j * CAP : (j + 1) * CAP], -1)
            for j in range(RADIUS)
        ],
        axis=1,
    )
    both = crossed_ref[...].astype(F32)
    weighted = flux(air, both[:NF], scale_ref[...], both[NF : NF + 1], index >= 0)
    column = jnp.where(low, cols_ref[:count, 1:2], cols_ref[last : last + count, 1:2])
    atm_ref[...] = near_ref[...] + summed_onto(halves(weighted), one_hot_rows(column, ATM))
    atm_copy = pltpu.make_async_copy(atm_ref, atm_hbm, sems.at[1])
    atm_copy.start()
    ocn_copy.wait()
    atm_copy.wait()


def call(kernel, name, ins, outs, scratch=(), space=pltpu.VMEM, first=pltpu.VMEM, rest=pltpu.VMEM):
    specs = [SMEM] + [pl.BlockSpec(memory_space=space)] * (len(ins) - 1)
    single = len(outs) == 1
    shapes = [jax.ShapeDtypeStruct(s, d) for s, d in outs]
    return pl.pallas_call(
        kernel,
        out_shape=shapes[0] if single else shapes,
        in_specs=specs,
        out_specs=pl.BlockSpec(memory_space=first) if single else [pl.BlockSpec(memory_space=x) for x in [first] + [rest] * (len(outs) - 1)],
        scratch_shapes=list(scratch),
        name=name,
        compiler_params=pltpu.CompilerParams(vmem_limit_bytes=24 * 1024 * 1024),
    )(*ins)


def on_device(
    planes, atm_fields, ocn_fields, transfer_scale, atmosphere_slots, ocn_slots, xc_ocean, xc_area, xc_theta
):
    w = lax.axis_index("w")
    place = w.reshape(1).astype(jnp.int32)
    table = pltpu.VMEM((NF, EPAD), BF)
    given = (
        ocn_fields,
        ocn_slots[0],
        atm_fields,
        atmosphere_slots.reshape(ROWS, 1, CAP),
        xc_ocean[0],
        xc_theta,
        xc_area,
        transfer_scale[None, :],
    )
    sending, own, cross, wide, air, entry_row, slot_row, ocean, theta, area, scale = call(
        send_kernel,
        "send",
        (place, *(pltpu.with_memory_space_constraint(x, pltpu.HBM) for x in given)),
        [
            ((Y, NF, OCAP), BF),
            ((W, NF, CAP), BF),
            ((NF, RADIUS * CAP), BF),
            ((NF, WIDE), BF),
            ((NF, W * CAP), BF),
            ((1, EPAD), jnp.int32),
            ((1, W * CAP), jnp.int32),
            ((2, SLOTS), jnp.int32),
            ((1, SLOTS), BF),
            ((1, SLOTS), BF),
            ((NF, 1), F32),
        ],
        [
            pltpu.VMEM((NF, OCN), BF),
            pltpu.VMEM((Y, OCAP), jnp.int32),
            pltpu.VMEM((NF, ATM), BF),
            pltpu.VMEM((ROWS, 1, CAP), jnp.int32),
            pltpu.VMEM((1, NF), F32),
            pltpu.VMEM((Y, PAD), jnp.int32),
            pltpu.VMEM((W, 1, CAP), jnp.int32),
            pltpu.VMEM((Y, NF, OCAP), BF),
            pltpu.SemaphoreType.DMA((9,)),
        ],
        pltpu.HBM,
        pltpu.HBM,
    )
    cols = call(
        columns_kernel,
        "columns",
        (place, entry_row, slot_row, ocean),
        [((EPAD, 8), jnp.int32)],
        [pltpu.VMEM((8, EPAD), jnp.int32)],
    )
    up, down = [], []
    for z in range(planes):
        for v in range(W):
            here, above, below = z * W + v, (z + 1) % planes * W + v, (z - 1) % planes * W + v
            if v >= W - RADIUS:
                up.append((here, above))
                down.append((here, below))
            if v < RADIUS:
                up.append((here, below))
                down.append((here, above))
    entries = lax.all_to_all(sending, "ocn", 0, 0, tiled=True)
    rising = [pair for pair in up if pair[0] % W >= W // 2]
    falling = [pair for pair in up if pair[0] % W < W // 2]
    crossed_up = lax.ppermute(wide, ("z", "w"), rising)
    crossed_down = lax.ppermute(cross, ("z", "w"), falling)
    sea, message = call(
        make_message_kernel,
        "make_message",
        (place, entries, ocean, theta, area, own, cols),
        [((NF, SLOTS), BF), ((W, MSG, 2 * CAP), BF)],
        [table],
    )
    message = call(
        add_crossed_kernel,
        "add_crossed",
        (place, message, crossed_up, crossed_down),
        [((W, MSG, 2 * CAP), BF)],
    )
    got = lax.all_to_all(message, "w", 0, 0, tiled=True)
    entry, away = call(
        entry_flux_kernel,
        "entry_flux",
        (place, got, sea, ocean, theta, area, scale, cols),
        [((Y, NF, OCAP), BF), ((MSG, RADIUS * CAP), BF)],
    )
    returned = lax.all_to_all(entry, "ocn", 0, 0, tiled=True)
    back = lax.ppermute(away, ("z", "w"), down)
    near = call(near_flux_kernel, "near_flux", (place, got, air, slot_row, scale, cols), [((NF, ATM), F32)])
    ocn_flux = call(ocn_flux_kernel, "ocn_flux", (place, returned, cols), [((NF, OCN), F32)], [table])
    return call(
        last_kernel,
        "last",
        (place, ocn_flux, near, back, air, slot_row, scale, cols),
        [((NF, ATM), F32), ((NF, OCN), F32)],
        [pltpu.VMEM((NF, ATM), F32), pltpu.SemaphoreType.DMA((2,))],
        first=pltpu.HBM,
        rest=pltpu.HBM,
    )


def solution(mesh):
    n_atm, n_ocn = mesh.shape["atm"], mesh.shape["ocn"]
    planes = n_atm // W
    split = Mesh(mesh.devices.reshape(planes, W, n_ocn), ("z", "w", "ocn"))
    every = ("z", "w", "ocn")
    placed = (
        P(None, every),
        P(None, every),
        P(),
        P(every, None, None),
        P(every, None, None),
        P(every, None, None),
        P(every, None),
        P(every, None),
    )
    return jax.shard_map(
        functools.partial(on_device, planes),
        mesh=split,
        in_specs=placed,
        out_specs=(P(None, every), P(None, every)),
        check_vma=False,
    )
```

```python
import functools
import jax
import jax.numpy as jnp
from jax import lax
from jax.experimental import pallas as pl
from jax.experimental.pallas import tpu as pltpu
from jax.sharding import Mesh, PartitionSpec as P

NF = 64
RADIUS = 3
CAP = 64
ITERS = 3
ROWS = 7
SLOTS = ROWS * CAP
W = 8
Y = 8
OCAP = 96
PAD = 128
EPAD = Y * PAD
ATM = 256
OCN = 384
MSG = NF + 8
SIDE = PAD - OCAP
PACK = NF * OCAP // PAD
WIDE = 1536
BF = jnp.bfloat16
F32 = jnp.float32
VMEM = pl.BlockSpec(memory_space=pltpu.VMEM)
SMEM = pl.BlockSpec(memory_space=pltpu.SMEM)


def one_hot(rows, index):
    ids = lax.broadcasted_iota(jnp.int32, (rows, index.shape[1]), 0)
    return jnp.where(ids == index, 1.0, 0.0).astype(BF)


def padded_entries(index):
    moved = index
    for o in range(1, Y):
        moved = moved + jnp.where(index >= o * OCAP, PAD - OCAP, 0)
    return moved


def pack(ref, o, values):
    ref[o, :, :OCAP] = values[:PACK].astype(BF)
    beside = [values[PACK:, j * SIDE : (j + 1) * SIDE] for j in range(OCAP // SIDE)]
    ref[o, :, OCAP:] = jnp.concatenate(beside, axis=0).astype(BF)


def unpack(table, ref):
    table[...] = jnp.zeros((NF, EPAD), BF)
    for o in range(Y):
        lanes = slice(o * PAD, o * PAD + OCAP)
        table[:PACK, lanes] = ref[o, :, :OCAP]
        beside = ref[o, :, OCAP:].astype(F32)
        rows = NF - PACK
        parts = [beside[j * rows : (j + 1) * rows] for j in range(OCAP // SIDE)]
        table[PACK:, lanes] = jnp.concatenate(parts, axis=1).astype(BF)


def flux(air, sea, scale, area, live):
    du = air[1:2] - sea[1:2]
    dv = air[2:3] - sea[2:3]
    square = du * du + dv * dv + 0.25
    speed = jnp.sqrt(square)
    contrast = air[0:1] - sea[0:1]
    coeff = jnp.ones_like(speed)
    for step in range(ITERS):
        coeff = 1.5 - 0.8 * jnp.tanh(0.3 * contrast * coeff / (speed * speed))
    factor = jnp.where(live, area * (coeff * speed), 0.0)
    return factor * (scale * (air - sea))


def halves(values):
    high = values.astype(BF)
    low = (values - high.astype(F32)).astype(BF)
    return jnp.concatenate([high, low], axis=0)


def one_hot_rows(index, columns):
    ids = lax.broadcasted_iota(jnp.int32, (index.shape[0], columns), 1)
    return jnp.where(ids == index, 1.0, 0.0).astype(BF)


def summed_onto(values, picker):
    both = jnp.dot(values, picker, preferred_element_type=F32)
    return both[:NF] + both[NF:]


def send_kernel(
    place_ref, ocn_hbm, entries_hbm, atm_hbm, slots_hbm, ocean_hbm, theta_hbm, area_hbm, scale_hbm,
    out_hbm, own_ref, cross_ref, wide_ref, air_ref, entry_row_ref, slot_row_ref, ocean_ref, theta_ref, area_ref, scale_ref,
    ocn_ref, entries_ref, atm_ref, slots_ref, row_ref, padded, placed, out_ref, sems,
):
    w = place_ref[0]
    pairs = [
        (entries_hbm, entries_ref),
        (ocn_hbm, ocn_ref),
        (slots_hbm, slots_ref),
        (atm_hbm, atm_ref),
        (ocean_hbm, ocean_ref),
        (theta_hbm, theta_ref),
        (area_hbm, area_ref),
        (scale_hbm, row_ref),
    ]
    copies = [pltpu.make_async_copy(a, b, sems.at[i]) for i, (a, b) in enumerate(pairs)]
    for copy in copies:
        copy.start()
    padded[...] = jnp.full((Y, PAD), -1, jnp.int32)
    copies[0].wait()
    padded[:, :OCAP] = entries_ref[...]
    index = jnp.concatenate([padded[o : o + 1, :] for o in range(Y)], axis=1)
    entry_row_ref[...] = index
    picker = one_hot(OCN, index)
    copies[1].wait()
    picked = jnp.dot(ocn_ref[...], picker, preferred_element_type=F32)
    for o in range(Y):
        pack(out_ref, o, picked[:, o * PAD : o * PAD + OCAP])
    leave = pltpu.make_async_copy(out_ref, out_hbm, sems.at[len(pairs)])
    leave.start()
    copies[2].wait()
    for k in range(ROWS):
        placed[lax.rem(w + (k - RADIUS + W), W)] = slots_ref[k]
    placed[lax.rem(w + W // 2, W)] = jnp.full((1, CAP), -1, jnp.int32)
    index = jnp.concatenate([placed[p] for p in range(W)], axis=1)
    slot_row_ref[...] = index
    picker = one_hot(ATM, index)
    copies[3].wait()
    air = jnp.dot(atm_ref[...], picker, preferred_element_type=F32)
    crossing = jnp.where(w >= W // 2, air[:, : RADIUS * CAP], air[:, (W - RADIUS) * CAP :]).astype(BF)
    cross_ref[...] = crossing
    wide_ref[...] = jnp.zeros((NF, WIDE), BF)
    wide_ref[:, : RADIUS * CAP] = crossing
    air_ref[...] = air.astype(BF)
    for p in range(W):
        own_ref[p] = air[:, p * CAP : (p + 1) * CAP].astype(BF)
    for copy in copies[4:]:
        copy.wait()
    rows = lax.broadcasted_iota(jnp.int32, (NF, NF), 0)
    lanes = lax.broadcasted_iota(jnp.int32, (NF, NF), 1)
    scale_ref[...] = jnp.sum(jnp.where(rows == lanes, row_ref[...], 0.0), axis=1, keepdims=True)
    leave.wait()


def columns_kernel(place_ref, entries_ref, slots_ref, ocean_ref, out_ref, rows_ref):
    rows_ref[...] = jnp.full((8, EPAD), -1, jnp.int32)
    rows_ref[0:1] = entries_ref[...]
    rows_ref[1:2, : W * CAP] = slots_ref[...]
    rows_ref[2:4, :SLOTS] = padded_entries(ocean_ref[...])
    out_ref[...] = rows_ref[...].T


def make_message_kernel(
    place_ref, entries_ref, ocean_ref, theta_ref, area_ref, own_ref, cols_ref, sea_ref, msg_ref, table
):
    w = place_ref[0]
    unpack(table, entries_ref)
    index = padded_entries(ocean_ref[...])
    entries = table[...]
    first = jnp.dot(entries, one_hot(EPAD, index[0:1]), preferred_element_type=F32)
    second = jnp.dot(entries, one_hot(EPAD, index[1:2]), preferred_element_type=F32)
    theta = theta_ref[...].astype(F32)
    sea = theta * first + (1.0 - theta) * second
    sea_ref[...] = sea.astype(BF)
    area = jnp.broadcast_to(area_ref[...].astype(F32), (MSG - NF, SLOTS))
    both = jnp.concatenate([sea, area], axis=0)
    for p in range(W):
        msg_ref[p, :, :CAP] = jnp.concatenate([own_ref[p], jnp.zeros((MSG - NF, CAP), BF)], axis=0)
    for k in range(ROWS):
        msg_ref[lax.rem(w + (RADIUS - k + W), W), :, CAP:] = both[:, k * CAP : (k + 1) * CAP].astype(BF)
    msg_ref[lax.rem(w + W // 2, W), :, CAP:] = jnp.zeros((MSG, CAP), BF)


def add_crossed_kernel(place_ref, msg_ref, up_ref, down_ref, out_ref):
    w = place_ref[0]
    for p in range(W):
        out_ref[p] = msg_ref[p]
        if p < RADIUS or p >= W - RADIUS:
            j = p if p < RADIUS else p - (W - RADIUS)
            there = up_ref if p < RADIUS else down_ref
            mine = msg_ref[p, :NF, :CAP]
            mine = jnp.where(jnp.abs(p - w) > W // 2, there[:, j * CAP : (j + 1) * CAP], mine)
            out_ref[p, :NF, :CAP] = mine


def entry_flux_kernel(
    place_ref, got_ref, sea_ref, ocean_ref, theta_ref, area_ref, scale_ref, cols_ref, out_ref, cross_ref
):
    w = place_ref[0]
    air = jnp.concatenate(
        [got_ref[lax.rem(w + (RADIUS - k + W), W), :NF, :CAP].astype(F32) for k in range(ROWS)], axis=1
    )
    weighted = flux(
        air, sea_ref[...].astype(F32), scale_ref[...], area_ref[...].astype(F32), ocean_ref[0:1, :] >= 0
    )
    theta = theta_ref[...].astype(F32)
    total = summed_onto(halves(theta * weighted), one_hot_rows(cols_ref[:SLOTS, 2:3], EPAD))
    total = total + summed_onto(halves((1.0 - theta) * weighted), one_hot_rows(cols_ref[:SLOTS, 3:4], EPAD))
    for o in range(Y):
        pack(out_ref, o, total[:, o * PAD : o * PAD + OCAP])
    first = jnp.where(w < W // 2, W - RADIUS, 0)
    crossing = [got_ref[first + j, :, CAP:].astype(F32) for j in range(RADIUS)]
    cross_ref[...] = jnp.concatenate(crossing, axis=1).astype(BF)


def near_flux_kernel(place_ref, got_ref, air_ref, slots_ref, scale_ref, cols_ref, out_ref):
    w = place_ref[0]
    both = jnp.concatenate([got_ref[p, :, CAP:].astype(F32) for p in range(W)], axis=1)
    slots = slots_ref[...]
    index = jnp.concatenate(
        [jnp.where(jnp.abs(p - w) > W // 2, -1, slots[:, p * CAP : (p + 1) * CAP]) for p in range(W)], axis=1
    )
    weighted = flux(
        air_ref[...].astype(F32), both[:NF], scale_ref[...], both[NF : NF + 1], index >= 0
    )
    out_ref[...] = summed_onto(halves(weighted), one_hot_rows(cols_ref[: W * CAP, 1:2], ATM))


def ocn_flux_kernel(place_ref, returned_ref, cols_ref, out_ref, table):
    unpack(table, returned_ref)
    out_ref[...] = jnp.dot(table[...], one_hot_rows(cols_ref[:, 0:1], OCN), preferred_element_type=F32)


def last_kernel(
    place_ref, ocn_ref, near_ref, crossed_ref, air_ref, slots_ref, scale_ref, cols_ref,
    atm_hbm, ocn_hbm, atm_ref, sems,
):
    w = place_ref[0]
    ocn_copy = pltpu.make_async_copy(ocn_ref, ocn_hbm, sems.at[0])
    ocn_copy.start()
    low = w >= W // 2
    count = RADIUS * CAP
    last = (W - RADIUS) * CAP
    air = jnp.where(low, air_ref[:, :count].astype(F32), air_ref[:, last:].astype(F32))
    slots = jnp.where(low, slots_ref[:, :count], slots_ref[:, last:])
    first = jnp.where(low, 0, W - RADIUS)
    index = jnp.concatenate(
        [
            jnp.where(jnp.abs(first + j - w) > W // 2, slots[:, j * CAP : (j + 1) * CAP], -1)
            for j in range(RADIUS)
        ],
        axis=1,
    )
    both = crossed_ref[...].astype(F32)
    weighted = flux(air, both[:NF], scale_ref[...], both[NF : NF + 1], index >= 0)
    column = jnp.where(low, cols_ref[:count, 1:2], cols_ref[last : last + count, 1:2])
    atm_ref[...] = near_ref[...] + summed_onto(halves(weighted), one_hot_rows(column, ATM))
    atm_copy = pltpu.make_async_copy(atm_ref, atm_hbm, sems.at[1])
    atm_copy.start()
    ocn_copy.wait()
    atm_copy.wait()


def call(kernel, name, ins, outs, scratch=(), space=pltpu.VMEM, first=pltpu.VMEM, rest=pltpu.VMEM):
    specs = [SMEM] + [pl.BlockSpec(memory_space=space)] * (len(ins) - 1)
    single = len(outs) == 1
    shapes = [jax.ShapeDtypeStruct(s, d) for s, d in outs]
    return pl.pallas_call(
        kernel,
        out_shape=shapes[0] if single else shapes,
        in_specs=specs,
        out_specs=pl.BlockSpec(memory_space=first) if single else [pl.BlockSpec(memory_space=x) for x in [first] + [rest] * (len(outs) - 1)],
        scratch_shapes=list(scratch),
        name=name,
        compiler_params=pltpu.CompilerParams(vmem_limit_bytes=24 * 1024 * 1024),
    )(*ins)


def on_device(
    planes, atm_fields, ocn_fields, transfer_scale, atmosphere_slots, ocn_slots, xc_ocean, xc_area, xc_theta
):
    w = lax.axis_index("w")
    place = w.reshape(1).astype(jnp.int32)
    table = pltpu.VMEM((NF, EPAD), BF)
    given = (
        ocn_fields,
        ocn_slots[0],
        atm_fields,
        atmosphere_slots.reshape(ROWS, 1, CAP),
        xc_ocean[0],
        xc_theta,
        xc_area,
        transfer_scale[None, :],
    )
    sending, own, cross, wide, air, entry_row, slot_row, ocean, theta, area, scale = call(
        send_kernel,
        "send",
        (place, *(pltpu.with_memory_space_constraint(x, pltpu.HBM) for x in given)),
        [
            ((Y, PACK, PAD), BF),
            ((W, NF, CAP), BF),
            ((NF, RADIUS * CAP), BF),
            ((NF, WIDE), BF),
            ((NF, W * CAP), BF),
            ((1, EPAD), jnp.int32),
            ((1, W * CAP), jnp.int32),
            ((2, SLOTS), jnp.int32),
            ((1, SLOTS), BF),
            ((1, SLOTS), BF),
            ((NF, 1), F32),
        ],
        [
            pltpu.VMEM((NF, OCN), BF),
            pltpu.VMEM((Y, OCAP), jnp.int32),
            pltpu.VMEM((NF, ATM), BF),
            pltpu.VMEM((ROWS, 1, CAP), jnp.int32),
            pltpu.VMEM((1, NF), F32),
            pltpu.VMEM((Y, PAD), jnp.int32),
            pltpu.VMEM((W, 1, CAP), jnp.int32),
            pltpu.VMEM((Y, PACK, PAD), BF),
            pltpu.SemaphoreType.DMA((9,)),
        ],
        pltpu.HBM,
        pltpu.HBM,
    )
    cols = call(
        columns_kernel,
        "columns",
        (place, entry_row, slot_row, ocean),
        [((EPAD, 8), jnp.int32)],
        [pltpu.VMEM((8, EPAD), jnp.int32)],
    )
    up, down = [], []
    for z in range(planes):
        for v in range(W):
            here, above, below = z * W + v, (z + 1) % planes * W + v, (z - 1) % planes * W + v
            if v >= W - RADIUS:
                up.append((here, above))
                down.append((here, below))
            if v < RADIUS:
                up.append((here, below))
                down.append((here, above))
    entries = lax.all_to_all(sending, "ocn", 0, 0, tiled=True)
    rising = [pair for pair in up if pair[0] % W >= W // 2]
    falling = [pair for pair in up if pair[0] % W < W // 2]
    crossed_up = lax.ppermute(wide, ("z", "w"), rising)
    crossed_down = lax.ppermute(cross, ("z", "w"), falling)
    sea, message = call(
        make_message_kernel,
        "make_message",
        (place, entries, ocean, theta, area, own, cols),
        [((NF, SLOTS), BF), ((W, MSG, 2 * CAP), BF)],
        [table],
    )
    message = call(
        add_crossed_kernel,
        "add_crossed",
        (place, message, crossed_up, crossed_down),
        [((W, MSG, 2 * CAP), BF)],
    )
    got = lax.all_to_all(message, "w", 0, 0, tiled=True)
    entry, away = call(
        entry_flux_kernel,
        "entry_flux",
        (place, got, sea, ocean, theta, area, scale, cols),
        [((Y, PACK, PAD), BF), ((MSG, RADIUS * CAP), BF)],
    )
    returned = lax.all_to_all(entry, "ocn", 0, 0, tiled=True)
    back = lax.ppermute(away, ("z", "w"), down)
    near = call(near_flux_kernel, "near_flux", (place, got, air, slot_row, scale, cols), [((NF, ATM), F32)])
    ocn_flux = call(ocn_flux_kernel, "ocn_flux", (place, returned, cols), [((NF, OCN), F32)], [table])
    return call(
        last_kernel,
        "last",
        (place, ocn_flux, near, back, air, slot_row, scale, cols),
        [((NF, ATM), F32), ((NF, OCN), F32)],
        [pltpu.VMEM((NF, ATM), F32), pltpu.SemaphoreType.DMA((2,))],
        first=pltpu.HBM,
        rest=pltpu.HBM,
    )


def solution(mesh):
    n_atm, n_ocn = mesh.shape["atm"], mesh.shape["ocn"]
    planes = n_atm // W
    split = Mesh(mesh.devices.reshape(planes, W, n_ocn), ("z", "w", "ocn"))
    every = ("z", "w", "ocn")
    placed = (
        P(None, every),
        P(None, every),
        P(),
        P(every, None, None),
        P(every, None, None),
        P(every, None, None),
        P(every, None),
        P(every, None),
    )
    return jax.shard_map(
        functools.partial(on_device, planes),
        mesh=split,
        in_specs=placed,
        out_specs=(P(None, every), P(None, every)),
        check_vma=False,
    )
```

```python
import functools
import jax
import jax.numpy as jnp
from jax import lax
from jax.experimental import pallas as pl
from jax.experimental.pallas import tpu as pltpu
from jax.sharding import Mesh, PartitionSpec as P

NF = 64
RADIUS = 3
CAP = 64
ITERS = 3
ROWS = 7
SLOTS = ROWS * CAP
W = 8
Y = 8
OCAP = 96
PAD = 128
EPAD = Y * PAD
ATM = 256
OCN = 384
MSG = NF + 8
SIDE = PAD - OCAP
PACK = NF * OCAP // PAD
WIDE = 1536
BF = jnp.bfloat16
F32 = jnp.float32
VMEM = pl.BlockSpec(memory_space=pltpu.VMEM)
SMEM = pl.BlockSpec(memory_space=pltpu.SMEM)


def one_hot(rows, index):
    ids = lax.broadcasted_iota(jnp.int32, (rows, index.shape[1]), 0)
    return jnp.where(ids == index, 1.0, 0.0).astype(BF)


def padded_entries(index):
    moved = index
    for o in range(1, Y):
        moved = moved + jnp.where(index >= o * OCAP, PAD - OCAP, 0)
    return moved


def pack(ref, o, values):
    lanes = lax.broadcasted_iota(jnp.int32, (PACK, PAD), 1)
    last = values[PACK:]
    beside = [pltpu.roll(last, OCAP - j * SIDE, 1) for j in range(OCAP // SIDE)]
    ref[o] = jnp.where(lanes < OCAP, values[:PACK], jnp.concatenate(beside, axis=0)).astype(BF)


def unpack(table, ref):
    rows = NF - PACK
    lanes = lax.broadcasted_iota(jnp.int32, (rows, PAD), 1)
    for o in range(Y):
        block = slice(o * PAD, (o + 1) * PAD)
        table[:PACK, block] = ref[o]
        last = jnp.zeros((rows, PAD), F32)
        for j in range(OCAP // SIDE):
            there = pltpu.roll(ref[o, j * rows : (j + 1) * rows, :].astype(F32), (j + 1) * SIDE, 1)
            last = jnp.where((lanes >= j * SIDE) & (lanes < (j + 1) * SIDE), there, last)
        table[PACK:, block] = last.astype(BF)


def flux(air, sea, scale, area, live):
    du = air[1:2] - sea[1:2]
    dv = air[2:3] - sea[2:3]
    square = du * du + dv * dv + 0.25
    speed = jnp.sqrt(square)
    contrast = air[0:1] - sea[0:1]
    coeff = jnp.ones_like(speed)
    for step in range(ITERS):
        coeff = 1.5 - 0.8 * jnp.tanh(0.3 * contrast * coeff / (speed * speed))
    factor = jnp.where(live, area * (coeff * speed), 0.0)
    return factor * (scale * (air - sea))


def halves(values):
    high = values.astype(BF)
    low = (values - high.astype(F32)).astype(BF)
    return jnp.concatenate([high, low], axis=0)


def one_hot_rows(index, columns):
    ids = lax.broadcasted_iota(jnp.int32, (index.shape[0], columns), 1)
    return jnp.where(ids == index, 1.0, 0.0).astype(BF)


def summed_onto(values, picker):
    both = jnp.dot(values, picker, preferred_element_type=F32)
    return both[:NF] + both[NF:]


def send_kernel(
    place_ref, ocn_hbm, entries_hbm, atm_hbm, slots_hbm, ocean_hbm, theta_hbm, area_hbm, scale_hbm,
    out_hbm, own_ref, cross_ref, wide_ref, air_ref, entry_row_ref, slot_row_ref, ocean_ref, theta_ref, area_ref, scale_ref,
    ocn_ref, entries_ref, atm_ref, slots_ref, row_ref, padded, placed, out_ref, sems,
):
    w = place_ref[0]
    pairs = [
        (entries_hbm, entries_ref),
        (ocn_hbm, ocn_ref),
        (slots_hbm, slots_ref),
        (atm_hbm, atm_ref),
        (ocean_hbm, ocean_ref),
        (theta_hbm, theta_ref),
        (area_hbm, area_ref),
        (scale_hbm, row_ref),
    ]
    copies = [pltpu.make_async_copy(a, b, sems.at[i]) for i, (a, b) in enumerate(pairs)]
    for copy in copies:
        copy.start()
    padded[...] = jnp.full((Y, PAD), -1, jnp.int32)
    copies[0].wait()
    padded[:, :OCAP] = entries_ref[...]
    index = jnp.concatenate([padded[o : o + 1, :] for o in range(Y)], axis=1)
    entry_row_ref[...] = index
    picker = one_hot(OCN, index)
    copies[1].wait()
    picked = jnp.dot(ocn_ref[...], picker, preferred_element_type=F32)
    for o in range(Y):
        pack(out_ref, o, picked[:, o * PAD : (o + 1) * PAD])
    leave = pltpu.make_async_copy(out_ref, out_hbm, sems.at[len(pairs)])
    leave.start()
    copies[2].wait()
    for k in range(ROWS):
        placed[lax.rem(w + (k - RADIUS + W), W)] = slots_ref[k]
    placed[lax.rem(w + W // 2, W)] = jnp.full((1, CAP), -1, jnp.int32)
    index = jnp.concatenate([placed[p] for p in range(W)], axis=1)
    slot_row_ref[...] = index
    picker = one_hot(ATM, index)
    copies[3].wait()
    air = jnp.dot(atm_ref[...], picker, preferred_element_type=F32)
    crossing = jnp.where(w >= W // 2, air[:, : RADIUS * CAP], air[:, (W - RADIUS) * CAP :]).astype(BF)
    cross_ref[...] = crossing
    wide_ref[...] = jnp.zeros((NF, WIDE), BF)
    wide_ref[:, : RADIUS * CAP] = crossing
    air_ref[...] = air.astype(BF)
    for p in range(W):
        own_ref[p] = air[:, p * CAP : (p + 1) * CAP].astype(BF)
    for copy in copies[4:]:
        copy.wait()
    rows = lax.broadcasted_iota(jnp.int32, (NF, NF), 0)
    lanes = lax.broadcasted_iota(jnp.int32, (NF, NF), 1)
    scale_ref[...] = jnp.sum(jnp.where(rows == lanes, row_ref[...], 0.0), axis=1, keepdims=True)
    leave.wait()


def columns_kernel(place_ref, entries_ref, slots_ref, ocean_ref, out_ref, rows_ref):
    rows_ref[...] = jnp.full((8, EPAD), -1, jnp.int32)
    rows_ref[0:1] = entries_ref[...]
    rows_ref[1:2, : W * CAP] = slots_ref[...]
    rows_ref[2:4, :SLOTS] = padded_entries(ocean_ref[...])
    out_ref[...] = rows_ref[...].T


def make_message_kernel(
    place_ref, entries_ref, ocean_ref, theta_ref, area_ref, own_ref, cols_ref, sea_ref, msg_ref, table
):
    w = place_ref[0]
    unpack(table, entries_ref)
    index = padded_entries(ocean_ref[...])
    entries = table[...]
    first = jnp.dot(entries, one_hot(EPAD, index[0:1]), preferred_element_type=F32)
    second = jnp.dot(entries, one_hot(EPAD, index[1:2]), preferred_element_type=F32)
    theta = theta_ref[...].astype(F32)
    sea = theta * first + (1.0 - theta) * second
    sea_ref[...] = sea.astype(BF)
    area = jnp.broadcast_to(area_ref[...].astype(F32), (MSG - NF, SLOTS))
    both = jnp.concatenate([sea, area], axis=0)
    for p in range(W):
        msg_ref[p, :, :CAP] = jnp.concatenate([own_ref[p], jnp.zeros((MSG - NF, CAP), BF)], axis=0)
    for k in range(ROWS):
        msg_ref[lax.rem(w + (RADIUS - k + W), W), :, CAP:] = both[:, k * CAP : (k + 1) * CAP].astype(BF)
    msg_ref[lax.rem(w + W // 2, W), :, CAP:] = jnp.zeros((MSG, CAP), BF)


def add_crossed_kernel(place_ref, msg_ref, up_ref, down_ref, out_ref):
    w = place_ref[0]
    for p in range(W):
        out_ref[p] = msg_ref[p]
        if p < RADIUS or p >= W - RADIUS:
            j = p if p < RADIUS else p - (W - RADIUS)
            there = up_ref if p < RADIUS else down_ref
            mine = msg_ref[p, :NF, :CAP]
            mine = jnp.where(jnp.abs(p - w) > W // 2, there[:, j * CAP : (j + 1) * CAP], mine)
            out_ref[p, :NF, :CAP] = mine


def entry_flux_kernel(
    place_ref, got_ref, sea_ref, ocean_ref, theta_ref, area_ref, scale_ref, cols_ref, out_ref, cross_ref
):
    w = place_ref[0]
    air = jnp.concatenate(
        [got_ref[lax.rem(w + (RADIUS - k + W), W), :NF, :CAP].astype(F32) for k in range(ROWS)], axis=1
    )
    weighted = flux(
        air, sea_ref[...].astype(F32), scale_ref[...], area_ref[...].astype(F32), ocean_ref[0:1, :] >= 0
    )
    theta = theta_ref[...].astype(F32)
    total = summed_onto(halves(theta * weighted), one_hot_rows(cols_ref[:SLOTS, 2:3], EPAD))
    total = total + summed_onto(halves((1.0 - theta) * weighted), one_hot_rows(cols_ref[:SLOTS, 3:4], EPAD))
    for o in range(Y):
        pack(out_ref, o, total[:, o * PAD : (o + 1) * PAD])
    first = jnp.where(w < W // 2, W - RADIUS, 0)
    crossing = [got_ref[first + j, :, CAP:].astype(F32) for j in range(RADIUS)]
    cross_ref[...] = jnp.concatenate(crossing, axis=1).astype(BF)


def near_flux_kernel(place_ref, got_ref, air_ref, slots_ref, scale_ref, cols_ref, out_ref):
    w = place_ref[0]
    both = jnp.concatenate([got_ref[p, :, CAP:].astype(F32) for p in range(W)], axis=1)
    slots = slots_ref[...]
    index = jnp.concatenate(
        [jnp.where(jnp.abs(p - w) > W // 2, -1, slots[:, p * CAP : (p + 1) * CAP]) for p in range(W)], axis=1
    )
    weighted = flux(
        air_ref[...].astype(F32), both[:NF], scale_ref[...], both[NF : NF + 1], index >= 0
    )
    out_ref[...] = summed_onto(halves(weighted), one_hot_rows(cols_ref[: W * CAP, 1:2], ATM))


def ocn_flux_kernel(place_ref, returned_ref, cols_ref, out_ref, table):
    unpack(table, returned_ref)
    out_ref[...] = jnp.dot(table[...], one_hot_rows(cols_ref[:, 0:1], OCN), preferred_element_type=F32)


def last_kernel(
    place_ref, ocn_ref, near_ref, crossed_ref, air_ref, slots_ref, scale_ref, cols_ref,
    atm_hbm, ocn_hbm, atm_ref, sems,
):
    w = place_ref[0]
    ocn_copy = pltpu.make_async_copy(ocn_ref, ocn_hbm, sems.at[0])
    ocn_copy.start()
    low = w >= W // 2
    count = RADIUS * CAP
    last = (W - RADIUS) * CAP
    air = jnp.where(low, air_ref[:, :count].astype(F32), air_ref[:, last:].astype(F32))
    slots = jnp.where(low, slots_ref[:, :count], slots_ref[:, last:])
    first = jnp.where(low, 0, W - RADIUS)
    index = jnp.concatenate(
        [
            jnp.where(jnp.abs(first + j - w) > W // 2, slots[:, j * CAP : (j + 1) * CAP], -1)
            for j in range(RADIUS)
        ],
        axis=1,
    )
    both = crossed_ref[...].astype(F32)
    weighted = flux(air, both[:NF], scale_ref[...], both[NF : NF + 1], index >= 0)
    column = jnp.where(low, cols_ref[:count, 1:2], cols_ref[last : last + count, 1:2])
    atm_ref[...] = near_ref[...] + summed_onto(halves(weighted), one_hot_rows(column, ATM))
    atm_copy = pltpu.make_async_copy(atm_ref, atm_hbm, sems.at[1])
    atm_copy.start()
    ocn_copy.wait()
    atm_copy.wait()


def call(kernel, name, ins, outs, scratch=(), space=pltpu.VMEM, first=pltpu.VMEM, rest=pltpu.VMEM):
    specs = [SMEM] + [pl.BlockSpec(memory_space=space)] * (len(ins) - 1)
    single = len(outs) == 1
    shapes = [jax.ShapeDtypeStruct(s, d) for s, d in outs]
    return pl.pallas_call(
        kernel,
        out_shape=shapes[0] if single else shapes,
        in_specs=specs,
        out_specs=pl.BlockSpec(memory_space=first) if single else [pl.BlockSpec(memory_space=x) for x in [first] + [rest] * (len(outs) - 1)],
        scratch_shapes=list(scratch),
        name=name,
        compiler_params=pltpu.CompilerParams(vmem_limit_bytes=24 * 1024 * 1024),
    )(*ins)


def on_device(
    planes, atm_fields, ocn_fields, transfer_scale, atmosphere_slots, ocn_slots, xc_ocean, xc_area, xc_theta
):
    w = lax.axis_index("w")
    place = w.reshape(1).astype(jnp.int32)
    table = pltpu.VMEM((NF, EPAD), BF)
    given = (
        ocn_fields,
        ocn_slots[0],
        atm_fields,
        atmosphere_slots.reshape(ROWS, 1, CAP),
        xc_ocean[0],
        xc_theta,
        xc_area,
        transfer_scale[None, :],
    )
    sending, own, cross, wide, air, entry_row, slot_row, ocean, theta, area, scale = call(
        send_kernel,
        "send",
        (place, *(pltpu.with_memory_space_constraint(x, pltpu.HBM) for x in given)),
        [
            ((Y, PACK, PAD), BF),
            ((W, NF, CAP), BF),
            ((NF, RADIUS * CAP), BF),
            ((NF, WIDE), BF),
            ((NF, W * CAP), BF),
            ((1, EPAD), jnp.int32),
            ((1, W * CAP), jnp.int32),
            ((2, SLOTS), jnp.int32),
            ((1, SLOTS), BF),
            ((1, SLOTS), BF),
            ((NF, 1), F32),
        ],
        [
            pltpu.VMEM((NF, OCN), BF),
            pltpu.VMEM((Y, OCAP), jnp.int32),
            pltpu.VMEM((NF, ATM), BF),
            pltpu.VMEM((ROWS, 1, CAP), jnp.int32),
            pltpu.VMEM((1, NF), F32),
            pltpu.VMEM((Y, PAD), jnp.int32),
            pltpu.VMEM((W, 1, CAP), jnp.int32),
            pltpu.VMEM((Y, PACK, PAD), BF),
            pltpu.SemaphoreType.DMA((9,)),
        ],
        pltpu.HBM,
        pltpu.HBM,
    )
    cols = call(
        columns_kernel,
        "columns",
        (place, entry_row, slot_row, ocean),
        [((EPAD, 8), jnp.int32)],
        [pltpu.VMEM((8, EPAD), jnp.int32)],
    )
    up, down = [], []
    for z in range(planes):
        for v in range(W):
            here, above, below = z * W + v, (z + 1) % planes * W + v, (z - 1) % planes * W + v
            if v >= W - RADIUS:
                up.append((here, above))
                down.append((here, below))
            if v < RADIUS:
                up.append((here, below))
                down.append((here, above))
    entries = lax.all_to_all(sending, "ocn", 0, 0, tiled=True)
    rising = [pair for pair in up if pair[0] % W >= W // 2]
    falling = [pair for pair in up if pair[0] % W < W // 2]
    crossed_up = lax.ppermute(wide, ("z", "w"), rising)
    crossed_down = lax.ppermute(cross, ("z", "w"), falling)
    sea, message = call(
        make_message_kernel,
        "make_message",
        (place, entries, ocean, theta, area, own, cols),
        [((NF, SLOTS), BF), ((W, MSG, 2 * CAP), BF)],
        [table],
    )
    message = call(
        add_crossed_kernel,
        "add_crossed",
        (place, message, crossed_up, crossed_down),
        [((W, MSG, 2 * CAP), BF)],
    )
    got = lax.all_to_all(message, "w", 0, 0, tiled=True)
    entry, away = call(
        entry_flux_kernel,
        "entry_flux",
        (place, got, sea, ocean, theta, area, scale, cols),
        [((Y, PACK, PAD), BF), ((MSG, RADIUS * CAP), BF)],
    )
    returned = lax.all_to_all(entry, "ocn", 0, 0, tiled=True)
    back = lax.ppermute(away, ("z", "w"), down)
    near = call(near_flux_kernel, "near_flux", (place, got, air, slot_row, scale, cols), [((NF, ATM), F32)])
    ocn_flux = call(ocn_flux_kernel, "ocn_flux", (place, returned, cols), [((NF, OCN), F32)], [table])
    return call(
        last_kernel,
        "last",
        (place, ocn_flux, near, back, air, slot_row, scale, cols),
        [((NF, ATM), F32), ((NF, OCN), F32)],
        [pltpu.VMEM((NF, ATM), F32), pltpu.SemaphoreType.DMA((2,))],
        first=pltpu.HBM,
        rest=pltpu.HBM,
    )


def solution(mesh):
    n_atm, n_ocn = mesh.shape["atm"], mesh.shape["ocn"]
    planes = n_atm // W
    split = Mesh(mesh.devices.reshape(planes, W, n_ocn), ("z", "w", "ocn"))
    every = ("z", "w", "ocn")
    placed = (
        P(None, every),
        P(None, every),
        P(),
        P(every, None, None),
        P(every, None, None),
        P(every, None, None),
        P(every, None),
        P(every, None),
    )
    return jax.shard_map(
        functools.partial(on_device, planes),
        mesh=split,
        in_specs=placed,
        out_specs=(P(None, every), P(None, every)),
        check_vma=False,
    )
```

```python
import functools
import jax
import jax.numpy as jnp
from jax import lax
from jax.experimental import pallas as pl
from jax.experimental.pallas import tpu as pltpu
from jax.sharding import Mesh, PartitionSpec as P

NF = 64
RADIUS = 3
CAP = 64
ITERS = 3
ROWS = 7
SLOTS = ROWS * CAP
W = 8
Y = 8
OCAP = 96
PAD = 128
EPAD = Y * PAD
ATM = 256
OCN = 384
MSG = NF + 8
SIDE = PAD - OCAP
PACK = NF * OCAP // PAD
WIDE = 1408
BF = jnp.bfloat16
F32 = jnp.float32
VMEM = pl.BlockSpec(memory_space=pltpu.VMEM)
SMEM = pl.BlockSpec(memory_space=pltpu.SMEM)


def one_hot(rows, index):
    ids = lax.broadcasted_iota(jnp.int32, (rows, index.shape[1]), 0)
    return jnp.where(ids == index, 1.0, 0.0).astype(BF)


def padded_entries(index):
    moved = index
    for o in range(1, Y):
        moved = moved + jnp.where(index >= o * OCAP, PAD - OCAP, 0)
    return moved


def pack(ref, o, values):
    lanes = lax.broadcasted_iota(jnp.int32, (PACK, PAD), 1)
    last = values[PACK:]
    beside = [pltpu.roll(last, OCAP - j * SIDE, 1) for j in range(OCAP // SIDE)]
    ref[o] = jnp.where(lanes < OCAP, values[:PACK], jnp.concatenate(beside, axis=0)).astype(BF)


def unpack(table, ref):
    rows = NF - PACK
    lanes = lax.broadcasted_iota(jnp.int32, (rows, PAD), 1)
    for o in range(Y):
        block = slice(o * PAD, (o + 1) * PAD)
        table[:PACK, block] = ref[o]
        last = jnp.zeros((rows, PAD), F32)
        for j in range(OCAP // SIDE):
            there = pltpu.roll(ref[o, j * rows : (j + 1) * rows, :].astype(F32), (j + 1) * SIDE, 1)
            last = jnp.where((lanes >= j * SIDE) & (lanes < (j + 1) * SIDE), there, last)
        table[PACK:, block] = last.astype(BF)


def flux(air, sea, scale, area, live):
    du = air[1:2] - sea[1:2]
    dv = air[2:3] - sea[2:3]
    square = du * du + dv * dv + 0.25
    speed = jnp.sqrt(square)
    contrast = air[0:1] - sea[0:1]
    coeff = jnp.ones_like(speed)
    for step in range(ITERS):
        coeff = 1.5 - 0.8 * jnp.tanh(0.3 * contrast * coeff / (speed * speed))
    factor = jnp.where(live, area * (coeff * speed), 0.0)
    return factor * (scale * (air - sea))


def halves(values):
    high = values.astype(BF)
    low = (values - high.astype(F32)).astype(BF)
    return jnp.concatenate([high, low], axis=0)


def one_hot_rows(index, columns):
    ids = lax.broadcasted_iota(jnp.int32, (index.shape[0], columns), 1)
    return jnp.where(ids == index, 1.0, 0.0).astype(BF)


def summed_onto(values, picker):
    both = jnp.dot(values, picker, preferred_element_type=F32)
    return both[:NF] + both[NF:]


def send_kernel(
    place_ref, ocn_hbm, entries_hbm, atm_hbm, slots_hbm, ocean_hbm, theta_hbm, area_hbm, scale_hbm,
    out_hbm, own_ref, cross_ref, wide_ref, air_ref, entry_row_ref, slot_row_ref, ocean_ref, theta_ref, area_ref, scale_ref,
    ocn_ref, entries_ref, atm_ref, slots_ref, row_ref, padded, placed, out_ref, sems,
):
    w = place_ref[0]
    pairs = [
        (entries_hbm, entries_ref),
        (ocn_hbm, ocn_ref),
        (slots_hbm, slots_ref),
        (atm_hbm, atm_ref),
        (ocean_hbm, ocean_ref),
        (theta_hbm, theta_ref),
        (area_hbm, area_ref),
        (scale_hbm, row_ref),
    ]
    copies = [pltpu.make_async_copy(a, b, sems.at[i]) for i, (a, b) in enumerate(pairs)]
    for copy in copies:
        copy.start()
    padded[...] = jnp.full((Y, PAD), -1, jnp.int32)
    copies[0].wait()
    padded[:, :OCAP] = entries_ref[...]
    index = jnp.concatenate([padded[o : o + 1, :] for o in range(Y)], axis=1)
    entry_row_ref[...] = index
    picker = one_hot(OCN, index)
    copies[1].wait()
    picked = jnp.dot(ocn_ref[...], picker, preferred_element_type=F32)
    for o in range(Y):
        pack(out_ref, o, picked[:, o * PAD : (o + 1) * PAD])
    leave = pltpu.make_async_copy(out_ref, out_hbm, sems.at[len(pairs)])
    leave.start()
    copies[2].wait()
    for k in range(ROWS):
        placed[lax.rem(w + (k - RADIUS + W), W)] = slots_ref[k]
    placed[lax.rem(w + W // 2, W)] = jnp.full((1, CAP), -1, jnp.int32)
    index = jnp.concatenate([placed[p] for p in range(W)], axis=1)
    slot_row_ref[...] = index
    picker = one_hot(ATM, index)
    copies[3].wait()
    air = jnp.dot(atm_ref[...], picker, preferred_element_type=F32)
    crossing = jnp.where(w >= W // 2, air[:, : RADIUS * CAP], air[:, (W - RADIUS) * CAP :]).astype(BF)
    cross_ref[...] = crossing
    wide_ref[...] = jnp.zeros((NF, WIDE), BF)
    wide_ref[:, : RADIUS * CAP] = crossing
    air_ref[...] = air.astype(BF)
    for p in range(W):
        own_ref[p] = air[:, p * CAP : (p + 1) * CAP].astype(BF)
    for copy in copies[4:]:
        copy.wait()
    rows = lax.broadcasted_iota(jnp.int32, (NF, NF), 0)
    lanes = lax.broadcasted_iota(jnp.int32, (NF, NF), 1)
    scale_ref[...] = jnp.sum(jnp.where(rows == lanes, row_ref[...], 0.0), axis=1, keepdims=True)
    leave.wait()


def columns_kernel(place_ref, entries_ref, slots_ref, ocean_ref, out_ref, rows_ref):
    rows_ref[...] = jnp.full((8, EPAD), -1, jnp.int32)
    rows_ref[0:1] = entries_ref[...]
    rows_ref[1:2, : W * CAP] = slots_ref[...]
    rows_ref[2:4, :SLOTS] = padded_entries(ocean_ref[...])
    out_ref[...] = rows_ref[...].T


def make_message_kernel(
    place_ref, entries_ref, ocean_ref, theta_ref, area_ref, own_ref, cols_ref, sea_ref, msg_ref, table
):
    w = place_ref[0]
    unpack(table, entries_ref)
    index = padded_entries(ocean_ref[...])
    entries = table[...]
    first = jnp.dot(entries, one_hot(EPAD, index[0:1]), preferred_element_type=F32)
    second = jnp.dot(entries, one_hot(EPAD, index[1:2]), preferred_element_type=F32)
    theta = theta_ref[...].astype(F32)
    sea = theta * first + (1.0 - theta) * second
    sea_ref[...] = sea.astype(BF)
    area = jnp.broadcast_to(area_ref[...].astype(F32), (MSG - NF, SLOTS))
    both = jnp.concatenate([sea, area], axis=0)
    for p in range(W):
        msg_ref[p, :, :CAP] = jnp.concatenate([own_ref[p], jnp.zeros((MSG - NF, CAP), BF)], axis=0)
    for k in range(ROWS):
        msg_ref[lax.rem(w + (RADIUS - k + W), W), :, CAP:] = both[:, k * CAP : (k + 1) * CAP].astype(BF)
    msg_ref[lax.rem(w + W // 2, W), :, CAP:] = jnp.zeros((MSG, CAP), BF)


def add_crossed_kernel(place_ref, msg_ref, up_ref, down_ref, out_ref):
    w = place_ref[0]
    for p in range(W):
        out_ref[p] = msg_ref[p]
        if p < RADIUS or p >= W - RADIUS:
            j = p if p < RADIUS else p - (W - RADIUS)
            there = up_ref if p < RADIUS else down_ref
            mine = msg_ref[p, :NF, :CAP]
            mine = jnp.where(jnp.abs(p - w) > W // 2, there[:, j * CAP : (j + 1) * CAP], mine)
            out_ref[p, :NF, :CAP] = mine


def entry_flux_kernel(
    place_ref, got_ref, sea_ref, ocean_ref, theta_ref, area_ref, scale_ref, cols_ref, out_ref, cross_ref
):
    w = place_ref[0]
    air = jnp.concatenate(
        [got_ref[lax.rem(w + (RADIUS - k + W), W), :NF, :CAP].astype(F32) for k in range(ROWS)], axis=1
    )
    weighted = flux(
        air, sea_ref[...].astype(F32), scale_ref[...], area_ref[...].astype(F32), ocean_ref[0:1, :] >= 0
    )
    theta = theta_ref[...].astype(F32)
    total = summed_onto(halves(theta * weighted), one_hot_rows(cols_ref[:SLOTS, 2:3], EPAD))
    total = total + summed_onto(halves((1.0 - theta) * weighted), one_hot_rows(cols_ref[:SLOTS, 3:4], EPAD))
    for o in range(Y):
        pack(out_ref, o, total[:, o * PAD : (o + 1) * PAD])
    first = jnp.where(w < W // 2, W - RADIUS, 0)
    crossing = [got_ref[first + j, :, CAP:].astype(F32) for j in range(RADIUS)]
    cross_ref[...] = jnp.concatenate(crossing, axis=1).astype(BF)


def near_flux_kernel(place_ref, got_ref, air_ref, slots_ref, scale_ref, cols_ref, out_ref):
    w = place_ref[0]
    both = jnp.concatenate([got_ref[p, :, CAP:].astype(F32) for p in range(W)], axis=1)
    slots = slots_ref[...]
    index = jnp.concatenate(
        [jnp.where(jnp.abs(p - w) > W // 2, -1, slots[:, p * CAP : (p + 1) * CAP]) for p in range(W)], axis=1
    )
    weighted = flux(
        air_ref[...].astype(F32), both[:NF], scale_ref[...], both[NF : NF + 1], index >= 0
    )
    out_ref[...] = summed_onto(halves(weighted), one_hot_rows(cols_ref[: W * CAP, 1:2], ATM))


def ocn_flux_kernel(place_ref, returned_ref, cols_ref, out_ref, table):
    unpack(table, returned_ref)
    out_ref[...] = jnp.dot(table[...], one_hot_rows(cols_ref[:, 0:1], OCN), preferred_element_type=F32)


def last_kernel(
    place_ref, ocn_ref, near_ref, crossed_ref, air_ref, slots_ref, scale_ref, cols_ref,
    atm_hbm, ocn_hbm, atm_ref, sems,
):
    w = place_ref[0]
    ocn_copy = pltpu.make_async_copy(ocn_ref, ocn_hbm, sems.at[0])
    ocn_copy.start()
    low = w >= W // 2
    count = RADIUS * CAP
    last = (W - RADIUS) * CAP
    air = jnp.where(low, air_ref[:, :count].astype(F32), air_ref[:, last:].astype(F32))
    slots = jnp.where(low, slots_ref[:, :count], slots_ref[:, last:])
    first = jnp.where(low, 0, W - RADIUS)
    index = jnp.concatenate(
        [
            jnp.where(jnp.abs(first + j - w) > W // 2, slots[:, j * CAP : (j + 1) * CAP], -1)
            for j in range(RADIUS)
        ],
        axis=1,
    )
    both = crossed_ref[...].astype(F32)
    weighted = flux(air, both[:NF], scale_ref[...], both[NF : NF + 1], index >= 0)
    column = jnp.where(low, cols_ref[:count, 1:2], cols_ref[last : last + count, 1:2])
    atm_ref[...] = near_ref[...] + summed_onto(halves(weighted), one_hot_rows(column, ATM))
    atm_copy = pltpu.make_async_copy(atm_ref, atm_hbm, sems.at[1])
    atm_copy.start()
    ocn_copy.wait()
    atm_copy.wait()


def call(kernel, name, ins, outs, scratch=(), space=pltpu.VMEM, first=pltpu.VMEM, rest=pltpu.VMEM):
    specs = [SMEM] + [pl.BlockSpec(memory_space=space)] * (len(ins) - 1)
    single = len(outs) == 1
    shapes = [jax.ShapeDtypeStruct(s, d) for s, d in outs]
    return pl.pallas_call(
        kernel,
        out_shape=shapes[0] if single else shapes,
        in_specs=specs,
        out_specs=pl.BlockSpec(memory_space=first) if single else [pl.BlockSpec(memory_space=x) for x in [first] + [rest] * (len(outs) - 1)],
        scratch_shapes=list(scratch),
        name=name,
        compiler_params=pltpu.CompilerParams(vmem_limit_bytes=24 * 1024 * 1024),
    )(*ins)


def on_device(
    planes, atm_fields, ocn_fields, transfer_scale, atmosphere_slots, ocn_slots, xc_ocean, xc_area, xc_theta
):
    w = lax.axis_index("w")
    place = w.reshape(1).astype(jnp.int32)
    table = pltpu.VMEM((NF, EPAD), BF)
    given = (
        ocn_fields,
        ocn_slots[0],
        atm_fields,
        atmosphere_slots.reshape(ROWS, 1, CAP),
        xc_ocean[0],
        xc_theta,
        xc_area,
        transfer_scale[None, :],
    )
    sending, own, cross, wide, air, entry_row, slot_row, ocean, theta, area, scale = call(
        send_kernel,
        "send",
        (place, *(pltpu.with_memory_space_constraint(x, pltpu.HBM) for x in given)),
        [
            ((Y, PACK, PAD), BF),
            ((W, NF, CAP), BF),
            ((NF, RADIUS * CAP), BF),
            ((NF, WIDE), BF),
            ((NF, W * CAP), BF),
            ((1, EPAD), jnp.int32),
            ((1, W * CAP), jnp.int32),
            ((2, SLOTS), jnp.int32),
            ((1, SLOTS), BF),
            ((1, SLOTS), BF),
            ((NF, 1), F32),
        ],
        [
            pltpu.VMEM((NF, OCN), BF),
            pltpu.VMEM((Y, OCAP), jnp.int32),
            pltpu.VMEM((NF, ATM), BF),
            pltpu.VMEM((ROWS, 1, CAP), jnp.int32),
            pltpu.VMEM((1, NF), F32),
            pltpu.VMEM((Y, PAD), jnp.int32),
            pltpu.VMEM((W, 1, CAP), jnp.int32),
            pltpu.VMEM((Y, PACK, PAD), BF),
            pltpu.SemaphoreType.DMA((9,)),
        ],
        pltpu.HBM,
        pltpu.HBM,
    )
    cols = call(
        columns_kernel,
        "columns",
        (place, entry_row, slot_row, ocean),
        [((EPAD, 8), jnp.int32)],
        [pltpu.VMEM((8, EPAD), jnp.int32)],
    )
    up, down = [], []
    for z in range(planes):
        for v in range(W):
            here, above, below = z * W + v, (z + 1) % planes * W + v, (z - 1) % planes * W + v
            if v >= W - RADIUS:
                up.append((here, above))
                down.append((here, below))
            if v < RADIUS:
                up.append((here, below))
                down.append((here, above))
    entries = lax.all_to_all(sending, "ocn", 0, 0, tiled=True)
    rising = [pair for pair in up if pair[0] % W >= W // 2]
    falling = [pair for pair in up if pair[0] % W < W // 2]
    crossed_up = lax.ppermute(wide, ("z", "w"), rising)
    crossed_down = lax.ppermute(cross, ("z", "w"), falling)
    sea, message = call(
        make_message_kernel,
        "make_message",
        (place, entries, ocean, theta, area, own, cols),
        [((NF, SLOTS), BF), ((W, MSG, 2 * CAP), BF)],
        [table],
    )
    message = call(
        add_crossed_kernel,
        "add_crossed",
        (place, message, crossed_up, crossed_down),
        [((W, MSG, 2 * CAP), BF)],
    )
    got = lax.all_to_all(message, "w", 0, 0, tiled=True)
    entry, away = call(
        entry_flux_kernel,
        "entry_flux",
        (place, got, sea, ocean, theta, area, scale, cols),
        [((Y, PACK, PAD), BF), ((MSG, RADIUS * CAP), BF)],
    )
    returned = lax.all_to_all(entry, "ocn", 0, 0, tiled=True)
    back = lax.ppermute(away, ("z", "w"), down)
    near = call(near_flux_kernel, "near_flux", (place, got, air, slot_row, scale, cols), [((NF, ATM), F32)])
    ocn_flux = call(ocn_flux_kernel, "ocn_flux", (place, returned, cols), [((NF, OCN), F32)], [table])
    return call(
        last_kernel,
        "last",
        (place, ocn_flux, near, back, air, slot_row, scale, cols),
        [((NF, ATM), F32), ((NF, OCN), F32)],
        [pltpu.VMEM((NF, ATM), F32), pltpu.SemaphoreType.DMA((2,))],
        first=pltpu.HBM,
        rest=pltpu.HBM,
    )


def solution(mesh):
    n_atm, n_ocn = mesh.shape["atm"], mesh.shape["ocn"]
    planes = n_atm // W
    split = Mesh(mesh.devices.reshape(planes, W, n_ocn), ("z", "w", "ocn"))
    every = ("z", "w", "ocn")
    placed = (
        P(None, every),
        P(None, every),
        P(),
        P(every, None, None),
        P(every, None, None),
        P(every, None, None),
        P(every, None),
        P(every, None),
    )
    return jax.shard_map(
        functools.partial(on_device, planes),
        mesh=split,
        in_specs=placed,
        out_specs=(P(None, every), P(None, every)),
        check_vma=False,
    )
```
